32 devices in a mesh: seq: 8 (over z, core), head: 4 (over y, x).
Axes of the slice: x: 2, y: 2, z: 4, core: 2. Of those that a mesh axis runs over, the one named last changes fastest.
Arguments:
- queries: bfloat16 [8192, 2048], P('seq', 'head'), may hold values from -1.5 to 1.5
- keys: bfloat16 [8192, 2048], P('seq', 'head'), may hold values from -1.5 to 1.5
- values: bfloat16 [8192, 2048], P('seq', 'head'), may hold values from -6 to 6
- log_decay: float32 [16, 8192], P('head', 'seq'), may hold values from -2 to 0, as said below
- out_weight: bfloat16 [2048, 2048], P(None, 'head'), may hold values from -0.125 to 0.125
- out_grad: bfloat16 [8192, 2048], P('seq', 'head'), may hold values from -0.75 to 0.75
Outputs:
- attended: bfloat16 [8192, 2048], P('seq', 'head')
- query_grad: bfloat16 [8192, 2048], P('seq', 'head')
- key_grad: bfloat16 [8192, 2048], P('seq', 'head')
- value_grad: bfloat16 [8192, 2048], P('seq', 'head')
- weight_grad: bfloat16 [2048, 2048], P('seq', 'head')
The draws below stay inside these ranges and needn't reach their ends.
Inputs may be any that keep to these rules, and one draw needn't show every extreme that they name: `log_decay`: natural logarithm of the factor by which a head's state is multiplied before the token's own key and value are added; always negative.
All inputs are finite; a program needn't handle non-finite values.
Results may differ from the reference program's by a relative error of at most 0.0069.
Values may be sent and summed in bfloat16 or wider, within the bound.
No kernel may reach another device: no remote copies, remote signals or barrier semaphores. Data moves between devices by JAX's collectives and lax.ppermute only.
A program may use at most 64 MiB of HBM per device.

```python
import math
import jax
import jax.numpy as jnp
from jax import lax

D = 2048
HEAD_COUNT = 16
DH = 128
TOK_DEV = 1024
SEQUENCE_TOKENS = 8192


def draw_log_decay(key, part):
    category_key, seed_key, block_random_key, jagged_random_key, location_key, spike_random_key = jax.random.split(key, 6)
    kinds = jax.random.randint(category_key, (HEAD_COUNT, 1), 0, 4)
    jagged_decay = jax.random.uniform(jagged_random_key, (HEAD_COUNT, SEQUENCE_TOKENS), jnp.float32, 0.4, 1.6)
    picker = jax.random.uniform(seed_key, (HEAD_COUNT, 1), jnp.float32, 0.0, 1.0)
    fast_rate = jnp.exp(math.log(1.0 / 50.0) + picker * math.log(50.0 / 30.0))
    middle_rate = (1.0 + 3.0 * picker) / TOK_DEV
    slow_rate = (0.2 + 0.6 * picker) / SEQUENCE_TOKENS
    decay_speed = jnp.where(kinds == 0, fast_rate, jnp.where(kinds == 1, middle_rate, slow_rate))
    block_count = SEQUENCE_TOKENS // TOK_DEV
    block_multiplier = jnp.exp(jax.random.uniform(block_random_key, (HEAD_COUNT, block_count), jnp.float32, -math.log(2.0), math.log(2.0)))
    block_multiplier = jnp.repeat(block_multiplier, TOK_DEV, axis=1)
    spots = jax.random.randint(location_key, (HEAD_COUNT, 3), 0, SEQUENCE_TOKENS)
    places = jnp.arange(SEQUENCE_TOKENS, dtype=jnp.int32)
    spike_positions = jnp.sum((places[None, None, :] == spots[:, :, None]).astype(jnp.float32), axis=1)
    spike_tokens = jax.random.uniform(spike_random_key, (HEAD_COUNT, SEQUENCE_TOKENS), jnp.float32, math.log(0.65), math.log(0.8))
    return (-decay_speed * block_multiplier * jagged_decay + spike_positions * spike_tokens).astype(jnp.float32)


def spiked(values, stream_key, source, target, blocks, factor):
    def block_of(position):
        return (jnp.arange(values.shape[position]) // (values.shape[position] // blocks)).reshape((-1,) + (1,) * (values.ndim - 1 - position))

    first = jax.random.permutation(stream_key, blocks)[block_of(target)]
    other_side = (block_of(target) + blocks // 2) % blocks
    return jnp.where((block_of(source) == first) | (block_of(source) == other_side), factor * values, values)


def block_levels(key, dims, pieces, least, top_value):
    gain, own = 1.0, jax.random.fold_in(key, 6)
    for axis_at, parts in pieces:
        heights = jnp.exp(jax.random.uniform(jax.random.fold_in(own, axis_at), (parts,), jnp.float32, least / len(pieces), top_value / len(pieces)))
        gain = gain * jnp.repeat(heights, dims[axis_at] // parts).reshape([-1 if axis == axis_at else 1 for axis in range(len(dims))])
    return gain


def gaussian(rng, extent, scale, bound, cuts=(), held_as=jnp.bfloat16):
    values = scale * jax.random.normal(rng, extent, jnp.float32)
    if cuts:
        values = values * block_levels(rng, extent, cuts, -0.22, 0.18)
    return jnp.clip(values, -bound, bound).astype(held_as)


def heavy_noise(stream_key, dims, width, limit, pieces, heavy, kind=jnp.bfloat16):
    values = width * jax.random.normal(stream_key, dims, jnp.float32)
    if pieces:
        values = values * block_levels(stream_key, dims, pieces, -0.22, 0.18)
    return jnp.clip(spiked(values, jax.random.fold_in(stream_key, 3), *heavy), -limit, limit).astype(kind)


def setup_inputs(seed: int = 0) -> dict:
    arg_keys = jax.random.split(jax.random.key(seed), 7)
    return {
        "queries": gaussian(arg_keys[0], (SEQUENCE_TOKENS, HEAD_COUNT * DH), 0.25, 1.5, ((0, 8), (1, 4))),
        "keys": gaussian(arg_keys[1], (SEQUENCE_TOKENS, HEAD_COUNT * DH), 0.25, 1.5, ((0, 8), (1, 4))),
        "values": gaussian(arg_keys[2], (SEQUENCE_TOKENS, HEAD_COUNT * DH), 1.0, 6.0, ((0, 8), (1, 4))),
        "log_decay": draw_log_decay(jax.random.fold_in(arg_keys[6], 71), 0),
        "out_weight": gaussian(arg_keys[4], (D, HEAD_COUNT * DH), (HEAD_COUNT * DH) ** -0.5, 0.125, ((1, 4),)),
        "out_grad": heavy_noise(arg_keys[5], (SEQUENCE_TOKENS, D), 0.125, 0.75, ((0, 8), (1, 4)), (0, 1, 8, 2.0)),
    }


HIGH = lax.Precision.HIGHEST

def to_low(array):
    return lax.optimization_barrier(array.astype(jnp.bfloat16)).astype(jnp.float32)

def one_head(inputs):
    query_rows, key_rows, value_rows, decay_rows, head_grad = inputs
    length = query_rows.shape[1]
    running = jnp.cumsum(decay_rows, axis=1)
    totals = running[:, -1]
    row_index = lax.broadcasted_iota(jnp.int32, (length, length), 0)
    col_index = lax.broadcasted_iota(jnp.int32, (length, length), 1)
    causal = (row_index >= col_index)[None]
    spread = running[:, :, None] - running[:, None, :]
    decay = jnp.where(causal, jnp.exp(jnp.where(causal, spread, 0.0)), 0.0)
    query_wide = query_rows.astype(jnp.float32)
    key_wide = key_rows.astype(jnp.float32)
    value_wide = value_rows.astype(jnp.float32)
    scores = jnp.einsum('ntd,nsd->nts', query_wide, key_wide, precision=HIGH)
    weights = (scores * decay).astype(jnp.bfloat16)
    tail_decay = jnp.exp(totals[:, None] - running)
    growth = jnp.exp(running)
    key_tail = to_low(key_wide * tail_decay[:, :, None])
    value_tail = to_low(value_wide * tail_decay[:, :, None])
    query_grown = to_low(query_wide * growth[:, :, None])
    update = jnp.einsum('nsd,nse->nde', key_tail, value_wide, precision=HIGH)

    def forward_step(state, item):
        total_now, block_state = item
        return (jnp.exp(total_now) * state + block_state, state)
    start_state = jnp.zeros(update.shape[1:], jnp.float32)
    _, incoming = lax.scan(forward_step, start_state, (totals, update))
    incoming_low = to_low(incoming)
    local_part = jnp.einsum('nts,nse->nte', weights.astype(jnp.float32), value_wide, precision=HIGH)
    carried = jnp.einsum('ntd,nde->nte', query_grown, incoming_low, precision=HIGH)
    mixed = local_part + carried
    root_mean = jnp.sqrt(lax.optimization_barrier(jnp.mean(mixed * mixed, axis=2, keepdims=True)) + 1e-05)
    normed = mixed / root_mean
    attended = normed.astype(jnp.bfloat16)
    norm_grad = (head_grad - normed * lax.optimization_barrier(jnp.mean(head_grad * normed, axis=2, keepdims=True))) / root_mean
    mixed_grad = norm_grad.astype(jnp.bfloat16)
    grad_wide = mixed_grad.astype(jnp.float32)
    grad_grown = to_low(grad_wide * growth[:, :, None])
    pair_grad = jnp.einsum('ntd,nsd->nts', grad_wide, value_wide, precision=HIGH)
    masked_grad = (pair_grad * decay).astype(jnp.bfloat16)
    back_update = jnp.einsum('ntd,nte->nde', query_grown, grad_wide, precision=HIGH)

    def backward_step(state, item):
        total_now, block_state = item
        return (block_state + jnp.exp(total_now) * state, state)
    _, outgoing = lax.scan(backward_step, start_state, (totals, back_update), reverse=True)
    outgoing_low = to_low(outgoing)
    masked_wide = masked_grad.astype(jnp.float32)
    weights_wide = weights.astype(jnp.float32)
    query_grad = jnp.einsum('nts,nsd->ntd', masked_wide, key_wide, precision=HIGH) + jnp.einsum('nte,nde->ntd', grad_grown, incoming_low, precision=HIGH)
    key_grad = jnp.einsum('nts,ntd->nsd', masked_wide, query_wide, precision=HIGH) + jnp.einsum('nse,nde->nsd', value_tail, outgoing_low, precision=HIGH)
    value_grad = jnp.einsum('nts,nte->nse', weights_wide, grad_wide, precision=HIGH) + jnp.einsum('nsd,nde->nse', key_tail, outgoing_low, precision=HIGH)
    return (attended, query_grad.astype(jnp.bfloat16), key_grad.astype(jnp.bfloat16), value_grad.astype(jnp.bfloat16))

def reference(queries, keys, values, log_decay, out_weight, out_grad):
    blocks = SEQUENCE_TOKENS // TOK_DEV

    def split_heads(array):
        return array.reshape(blocks, TOK_DEV, HEAD_COUNT, DH).transpose(2, 0, 1, 3)

    def join_heads(array):
        return array.transpose(1, 2, 0, 3).reshape(SEQUENCE_TOKENS, HEAD_COUNT * DH)
    head_grad = jnp.dot(out_grad, out_weight, preferred_element_type=jnp.float32)
    stacked = (split_heads(queries), split_heads(keys), split_heads(values), log_decay.reshape(HEAD_COUNT, blocks, TOK_DEV), split_heads(head_grad))
    results = lax.map(one_head, stacked)
    attended = join_heads(results[0])
    query_grad = join_heads(results[1])
    key_grad = join_heads(results[2])
    value_grad = join_heads(results[3])
    weight_grad = jnp.dot(out_grad.T, attended, preferred_element_type=jnp.float32).astype(jnp.bfloat16)
    return (attended, query_grad, key_grad, value_grad, weight_grad)
```

```python
import functools

import jax
import jax.numpy as jnp
from jax import lax
from jax.experimental import pallas as pl
from jax.experimental.pallas import tpu as pltpu
from jax.sharding import PartitionSpec as P

HIGH = lax.Precision.HIGHEST
F32 = jnp.float32
BF16 = jnp.bfloat16
VMEM = pl.BlockSpec(memory_space=pltpu.VMEM)
SMEM = pl.BlockSpec(memory_space=pltpu.SMEM)
NN = (((1,), (0,)), ((), ()))
NT = (((1,), (1,)), ((), ()))
TN = (((0,), (0,)), ((), ()))


def mm(left, right, dims):
    return lax.dot_general(left, right, dims, preferred_element_type=F32)


def call(body, outs, specs, flops, *args):
    shapes = [jax.ShapeDtypeStruct(shape, dtype) for shape, dtype in outs]
    moved = sum(a.size * a.dtype.itemsize for a in list(args) + shapes)
    return pl.pallas_call(
        body,
        out_shape=shapes,
        in_specs=specs,
        out_specs=[VMEM] * len(shapes),
        compiler_params=pltpu.CompilerParams(vmem_limit_bytes=32 * 1024 * 1024),
        cost_estimate=pl.CostEstimate(flops=flops, bytes_accessed=moved, transcendentals=0),
    )(*args)


def state_body(keys, values, log_decay, run_row, run_col, states, update):
    chunks, heads, size = run_row.shape
    width = states.shape[-1]
    source = lax.broadcasted_iota(jnp.int32, (size, size), 0)
    target = lax.broadcasted_iota(jnp.int32, (size, size), 1)
    upper = (source <= target).astype(F32)
    lower = (source >= target).astype(F32)
    for j in range(chunks):
        piece = log_decay[:, j * size : (j + 1) * size]
        run_row[j] = lax.dot_general(piece, upper, NN, precision=HIGH, preferred_element_type=F32)
        run_col[j] = lax.dot_general(lower, piece, NT, precision=HIGH, preferred_element_type=F32)
    for h in range(heads):
        cols = slice(h * width, (h + 1) * width)
        state = jnp.zeros((width, width), F32)
        for j in range(chunks):
            rows = slice(j * size, (j + 1) * size)
            run = run_col[j, :, h : h + 1]
            total = run[size - 1 : size, :]
            tail = (keys[rows, cols] * jnp.exp(total - run)).astype(BF16)
            states[h, j] = state
            state = state * jnp.exp(total) + mm(tail, values[rows, cols], TN)
        update[h] = state


def decay_of(run_row, run_col, j, h, causal):
    spread = run_col[j, :, h : h + 1] - run_row[j, h : h + 1, :]
    return jnp.exp(jnp.where(causal, spread, -jnp.inf))


def causal_mask(size):
    return lax.broadcasted_iota(jnp.int32, (size, size), 0) >= lax.broadcasted_iota(
        jnp.int32, (size, size), 1
    )


def local_body(queries, keys, values, run_row, run_col, states, weights, mixed):
    chunks, heads, size = run_row.shape
    width = states.shape[-1]
    causal = causal_mask(size)
    for h in range(heads):
        cols = slice(h * width, (h + 1) * width)
        for j in range(chunks):
            rows = slice(j * size, (j + 1) * size)
            query = queries[rows, cols]
            scores = mm(query, keys[rows, cols], NT)
            weight = (scores * decay_of(run_row, run_col, j, h, causal)).astype(BF16)
            weights[h, j] = weight
            grown = (query * jnp.exp(run_col[j, :, h : h + 1])).astype(BF16)
            mixed[rows, cols] = mm(weight, values[rows, cols], NN) + mm(
                grown, states[h, j].astype(BF16), NN
            )


def norm_body(mixed, queries, run_col, incoming, normed, attended, inverse):
    chunks, size, heads = run_col.shape
    width = incoming.shape[-1]
    for h in range(heads):
        cols = slice(h * width, (h + 1) * width)
        state = incoming[h].astype(BF16)
        before = jnp.zeros((1, 1), F32)
        for j in range(chunks):
            rows = slice(j * size, (j + 1) * size)
            run = run_col[j, :, h : h + 1]
            grown = (queries[rows, cols] * jnp.exp(run + before)).astype(BF16)
            total = mixed[rows, cols] + mm(grown, state, NN)
            scale = lax.rsqrt(jnp.mean(total * total, axis=1, keepdims=True) + 1e-05)
            inverse[j, :, h : h + 1] = scale
            total = total * scale
            normed[rows, cols] = total
            attended[rows, cols] = total.astype(BF16)
            before = before + run[size - 1 : size, :]


def head_grad_body(size, number, *refs):
    starts, weight = refs[0], refs[1]
    pieces, out = refs[2 : 2 + number], refs[2 + number]
    for t in range(out.shape[0] // size):
        rows = slice(t * size, (t + 1) * size)
        total = None
        for i, piece in enumerate(pieces):
            depth = piece.shape[1]
            start = pl.multiple_of(starts[i] * 64, 64)
            term = mm(piece[rows, :], weight[pl.ds(start, depth), :], NN)
            total = term if total is None else total + term
        out[rows, :] = total


def mixed_grad_body(number, *refs):
    starts, weight = refs[0], refs[1]
    pieces = refs[2 : 2 + number]
    partial, normed, inverse, queries, run_col = refs[2 + number : 7 + number]
    mixed_grad, states, update = refs[7 + number :]
    chunks, size, heads = run_col.shape
    width = update.shape[-1]
    for j in range(chunks):
        rows = slice(j * size, (j + 1) * size)
        total = partial[rows, :]
        for i, piece in enumerate(pieces):
            depth = piece.shape[1]
            start = pl.multiple_of(starts[i] * 64, 64)
            total = total + mm(piece[rows, :], weight[pl.ds(start, depth), :], NN)
        for h in range(heads):
            cols = slice(h * width, (h + 1) * width)
            grad = total[:, cols]
            unit = normed[rows, cols]
            mean = jnp.mean(grad * unit, axis=1, keepdims=True)
            grad = ((grad - unit * mean) * inverse[j, :, h : h + 1]).astype(BF16)
            mixed_grad[rows, cols] = grad
            grown = (queries[rows, cols] * jnp.exp(run_col[j, :, h : h + 1])).astype(BF16)
            states[h, j] = mm(grown, grad, TN)
    for h in range(heads):
        state = jnp.zeros((width, width), F32)
        for j in reversed(range(chunks)):
            own = states[h, j]
            states[h, j] = state
            state = own + state * jnp.exp(run_col[j, size - 1 : size, h : h + 1])
        update[h] = state


def back_body(
    queries, keys, values, mixed_grad, weights, run_row, run_col, states, incoming, back_states,
    query_grad, key_grad, value_grad,
):
    chunks, heads, size = run_row.shape
    width = states.shape[-1]
    causal = causal_mask(size)
    for h in range(heads):
        cols = slice(h * width, (h + 1) * width)
        before = jnp.zeros((1, 1), F32)
        for j in range(chunks):
            rows = slice(j * size, (j + 1) * size)
            run = run_col[j, :, h : h + 1]
            total = run[size - 1 : size, :]
            grad = mixed_grad[rows, cols]
            key, value = keys[rows, cols], values[rows, cols]
            pair = mm(grad, value, NT)
            masked = (pair * decay_of(run_row, run_col, j, h, causal)).astype(BF16)
            state = (states[h, j] + incoming[h] * jnp.exp(before)).astype(BF16)
            back_state = back_states[h, j].astype(BF16)
            grown = (grad * jnp.exp(run)).astype(BF16)
            query_grad[rows, cols] = (mm(masked, key, NN) + mm(grown, state, NT)).astype(BF16)
            tail = jnp.exp(total - run)
            key_grad[rows, cols] = mm(masked, queries[rows, cols], TN) + mm(
                (value * tail).astype(BF16), back_state, NT
            )
            value_grad[rows, cols] = mm(weights[h, j], grad, TN) + mm(
                (key * tail).astype(BF16), back_state, NN
            )
            before = before + total


def final_body(keys, values, run_col, outgoing, key_part, value_part, key_grad, value_grad):
    chunks, size, heads = run_col.shape
    width = outgoing.shape[-1]
    for h in range(heads):
        cols = slice(h * width, (h + 1) * width)
        state = outgoing[h].astype(BF16)
        after = jnp.zeros((1, 1), F32)
        for j in reversed(range(chunks)):
            rows = slice(j * size, (j + 1) * size)
            run = run_col[j, :, h : h + 1]
            after = after + run[size - 1 : size, :]
            tail = jnp.exp(after - run)
            key_grad[rows, cols] = (
                key_part[rows, cols] + mm((values[rows, cols] * tail).astype(BF16), state, NT)
            ).astype(BF16)
            value_grad[rows, cols] = (
                value_part[rows, cols] + mm((keys[rows, cols] * tail).astype(BF16), state, NN)
            ).astype(BF16)


def weight_grad_body(number, *refs):
    core = refs[0][0]
    pieces, attended, out = refs[1 : 1 + number], refs[1 + number], refs[2 + number]
    for i, (side, slot, piece, span) in enumerate(pieces_of(number, refs)):
        out[lax.rem(side + core, 2), slot] = mm(piece[:, span], attended[...], TN).astype(BF16)


def pieces_of(number, refs):
    raise NotImplementedError


class Chain:
    def __init__(self, totals, size):
        index = lax.axis_index("seq")
        self.chips = size // 2
        self.chip, self.core = index // 2, index % 2
        self.totals = totals
        heads = totals.shape[0]
        self.other = self.swap(totals)
        first = jnp.where(self.core == 0, totals, self.other)
        second = jnp.where(self.core == 0, self.other, totals)
        chip_total = first + second
        back = [self.shift(chip_total, k) for k in range(1, self.chips)]
        zero = jnp.zeros((heads,), F32)
        self.incoming, self.outgoing = [None] * self.chips, [None] * self.chips
        span = zero
        for k in range(1, self.chips):
            self.incoming[k] = jnp.where(k <= self.chip, jnp.exp(span), 0.0)
            span = span + back[k - 1]
        span = zero
        for k in reversed(range(1, self.chips)):
            self.outgoing[k] = jnp.where(k > self.chip, jnp.exp(span), 0.0)
            span = span + back[k - 1]

    def swap(self, value):
        return lax.ppermute(value, "seq", [(i, i ^ 1) for i in range(2 * self.chips)])

    def shift(self, value, k):
        pairs = [
            (i, (i // 2 + k) % self.chips * 2 + i % 2) for i in range(2 * self.chips)
        ]
        return lax.ppermute(value, "seq", pairs)

    def run(self, update, forward):
        low = update.astype(BF16)
        other = self.swap(low).astype(F32)
        near, far = jnp.exp(self.totals), jnp.exp(self.other)
        wide = lambda factor: factor[:, None, None]
        late = self.core == (1 if forward else 0)
        chip = jnp.where(late, update + wide(near) * other, other + wide(far) * update)
        chip = chip.astype(BF16)
        heads, rows, cols = chip.shape
        halves = chip.reshape(2, heads * rows // 2, cols)
        half = lax.dynamic_index_in_dim(halves, self.core, 0, keepdims=False)
        factors = self.incoming if forward else self.outgoing
        total = jnp.zeros(half.shape, F32)
        for k in range(1, self.chips):
            weight = jnp.repeat(factors[k], rows).reshape(2, heads * rows // 2)
            weight = lax.dynamic_index_in_dim(weight, self.core, 0, keepdims=False)
            total = total + weight[:, None] * self.shift(half, k).astype(F32)
        total = total.astype(BF16)
        theirs = self.swap(total)
        low_half = jnp.where(self.core == 0, total, theirs)
        high_half = jnp.where(self.core == 0, theirs, total)
        entering = jnp.concatenate([low_half, high_half]).reshape(chip.shape).astype(F32)
        return jnp.where(late, other + wide(far) * entering, entering)


def gather_pieces(out_grad, count):
    half = out_grad.shape[1] // 2
    move = lambda a, k: lax.ppermute(a, "head", [(i, i ^ k) for i in range(count)])
    low, high = out_grad[:, :half], out_grad[:, half:]
    x_low, y_high = move(low, 1), move(high, 2)
    diagonal_high, diagonal_low = move(y_high, 1), move(x_low, 2)
    x_high, y_low = move(high, 1), move(low, 2)
    early = [(0, 0, low), (0, 1, high), (1, 0, x_low), (2, 1, y_high)]
    late = [(3, 0, diagonal_low), (3, 1, diagonal_high), (1, 1, x_high), (2, 0, y_low)]
    return early, late


def reduce_rows(attended, group, chips, count):
    seq, head = lax.axis_index("seq"), lax.axis_index("head")
    chip, core = seq // 2, seq % 2
    sides = [[p for p in group if p[1] == side] for side in range(2)]
    product = lambda a: mm(a, attended, TN).astype(BF16)
    parts = [jnp.stack([product(p[2]) for p in side]) for side in sides]
    mine = jnp.where(core == 0, parts[0], parts[1])
    theirs = jnp.where(core == 0, parts[1], parts[0])
    pairs = [(i, i ^ 1) for i in range(2 * chips)]
    held = (mine.astype(F32) + lax.ppermute(theirs, "seq", pairs).astype(F32)).astype(BF16)

    def target(slot, side, where):
        return where ^ sides[side][slot][0]

    total = jnp.zeros(held.shape[1:], F32)
    for slot in range(2):
        goal = jnp.where(core == 0, target(slot, 0, head), target(slot, 1, head))
        total = total + jnp.where(chip == goal, held[slot].astype(F32), 0.0)
    for step in range(1, 4):
        moves, picks = [], []
        for s in range(2 * chips):
            for y in range(count):
                first, second = target(0, s % 2, y), target(1, s % 2, y)
                apart = first ^ second
                z = s // 2
                if z == first or z == second:
                    if step == apart:
                        goal, slot = (second, 1) if z == first else (first, 0)
                    else:
                        continue
                elif z ^ first == step:
                    goal, slot = first, 0
                elif z ^ second == step:
                    goal, slot = second, 1
                else:
                    continue
                moves.append((s * count + y, (goal * 2 + s % 2) * count + y))
                picks.append((s * count + y, slot))
        first = jnp.where(core == 0, target(0, 0, head), target(0, 1, head))
        sent = jnp.where((chip ^ first) == step, held[0], held[1])
        total = total + lax.ppermute(sent, ("seq", "head"), moves).astype(F32)
    return total


def on_device(seq_size, head_size, queries, keys, values, log_decay, out_weight, out_grad):
    length, columns = queries.shape
    heads = log_decay.shape[0]
    width = columns // heads
    size = 256 if length % 256 == 0 else length
    chunks = length // size
    head = lax.axis_index("head")
    chips = seq_size // 2
    near = head_size == 4 and chips == 4
    if near:
        early, late = gather_pieces(out_grad, head_size)
    else:
        whole = lax.all_gather(out_grad, "head", axis=1, tiled=True)
        early, late = [], []
    chain = Chain(jnp.sum(log_decay, axis=1), seq_size)
    square = heads * chunks * size * width * width * 2
    pairs = heads * chunks * size * size * width * 2
    run_row, run_col, states, update = call(
        state_body,
        [((chunks, heads, size), F32), ((chunks, size, heads), F32),
         ((heads, chunks, width, width), F32), ((heads, width, width), F32)],
        [VMEM] * 3, square, keys, values, log_decay,
    )
    incoming = chain.run(update, True)
    weights, mixed = call(
        local_body,
        [((heads, chunks, size, size), BF16), ((length, columns), F32)],
        [VMEM] * 6, 2 * pairs + square, queries, keys, values, run_row, run_col, states,
    )
    normed, attended, inverse = call(
        norm_body,
        [((length, columns), F32), ((length, columns), BF16), ((chunks, size, heads), F32)],
        [VMEM] * 4, square, mixed, queries, run_col, incoming,
    )

    def starts_of(group):
        block = out_grad.shape[1]
        return jnp.stack(
            [((head ^ k) * block + side * (block // 2)) // 64 for k, side, _ in group]
        ).astype(jnp.int32)

    if near:
        first = early + late[:2]
        partial, = call(
            functools.partial(head_grad_body, size, len(first)),
            [((length, columns), F32)],
            [SMEM] + [VMEM] * (1 + len(first)),
            2 * length * columns * out_weight.shape[0] * 3 // 4,
            starts_of(first), out_weight, *[p[2] for p in first],
        )
        last = late[2:]
    else:
        last = []
        partial = jnp.dot(whole, out_weight, preferred_element_type=F32)
    mixed_grad, back_states, back_update = call(
        functools.partial(mixed_grad_body, len(last)),
        [((length, columns), BF16), ((heads, chunks, width, width), F32),
         ((heads, width, width), F32)],
        [SMEM] + [VMEM] * (6 + len(last)),
        square + 2 * length * columns * out_weight.shape[0] // 4,
        starts_of(last) if last else jnp.zeros((1,), jnp.int32), out_weight,
        *[p[2] for p in last], partial, normed, inverse, queries, run_col,
    )
    outgoing = chain.run(back_update, False)
    query_grad, key_part, value_part = call(
        back_body,
        [((length, columns), BF16), ((length, columns), F32), ((length, columns), F32)],
        [VMEM] * 10, 4 * pairs + 3 * square,
        queries, keys, values, mixed_grad, weights, run_row, run_col, states, incoming,
        back_states,
    )
    key_grad, value_grad = call(
        final_body,
        [((length, columns), BF16)] * 2,
        [VMEM] * 6, 2 * square, keys, values, run_col, outgoing, key_part, value_part,
    )
    if near:
        weight_grad = reduce_rows(attended, early, chips, head_size) + reduce_rows(
            attended, late, chips, head_size
        )
    else:
        weight_grad = lax.psum_scatter(
            mm(whole, attended, TN), "seq", scatter_dimension=0, tiled=True
        )
    return attended, query_grad, key_grad, value_grad, weight_grad.astype(BF16)


def solution(mesh):
    block = P("seq", "head")
    return jax.shard_map(
        functools.partial(on_device, mesh.shape["seq"], mesh.shape["head"]),
        mesh=mesh,
        in_specs=(block, block, block, P("head", "seq"), P(None, "head"), block),
        out_specs=(block,) * 5,
        check_vma=False,
    )
```

```python
import functools

import jax
import jax.numpy as jnp
from jax import lax
from jax.experimental import pallas as pl
from jax.experimental.pallas import tpu as pltpu
from jax.sharding import PartitionSpec as P

HIGH = lax.Precision.HIGHEST
F32 = jnp.float32
BF16 = jnp.bfloat16
VMEM = pl.BlockSpec(memory_space=pltpu.VMEM)
ANY = pl.BlockSpec(memory_space=pl.ANY)
SMEM = pl.BlockSpec(memory_space=pltpu.SMEM)
NN = (((1,), (0,)), ((), ()))
NT = (((1,), (1,)), ((), ()))
TN = (((0,), (0,)), ((), ()))


def mm(left, right, dims):
    return lax.dot_general(left, right, dims, preferred_element_type=F32)


class Fetch:
    def __init__(self, source, buffer, semaphores, axis=1):
        self.buffer, self.axis = buffer, axis
        self.count = semaphores.shape[0]
        self.step = buffer.shape[axis] // self.count
        at = [
            (slice(None),) * axis + (slice(i * self.step, (i + 1) * self.step),)
            for i in range(self.count)
        ]
        self.copies = [
            pltpu.make_async_copy(source.at[p], buffer.at[p], semaphores.at[i])
            for i, p in enumerate(at)
        ]
        self.waiting = set(range(self.count))

    def __getitem__(self, index):
        span = index[self.axis] if isinstance(index, tuple) else slice(None)
        first, last = span.start or 0, span.stop or self.buffer.shape[self.axis]
        for i in sorted(self.waiting):
            if first < (i + 1) * self.step and i * self.step < last:
                self.copies[i].wait()
                self.waiting.discard(i)
        return self.buffer[index]


def start_all(*fetches):
    for i in range(max(f.count for f in fetches)):
        for f in fetches:
            if i < f.count:
                f.copies[i].start()


class Store(Fetch):
    def __init__(self, target, buffer, semaphores, axis=1):
        self.buffer, self.axis = buffer, axis
        self.count = semaphores.shape[0]
        self.step = buffer.shape[axis] // self.count
        at = [
            (slice(None),) * axis + (slice(i * self.step, (i + 1) * self.step),)
            for i in range(self.count)
        ]
        self.copies = [
            pltpu.make_async_copy(buffer.at[p], target.at[p], semaphores.at[i])
            for i, p in enumerate(at)
        ]

    def __setitem__(self, index, value):
        self.buffer[index] = value

    def send(self, i):
        self.copies[i].start()

    def finish(self):
        for copy in self.copies:
            copy.wait()


class Line:
    def __init__(self):
        self.last = None
        self.held = {}

    def call(self, body, outs, *args, scratch=(), scalars=0, fetch={}, store={}, raw=(), raw_out=()):
        fetch = {i: f if isinstance(f, tuple) else (f, 1) for i, f in fetch.items()}
        store = {i: f if isinstance(f, tuple) else (f, 1) for i, f in store.items()}
        shapes = [
            (pltpu.HBM if i in store or i in raw_out else jax.ShapeDtypeStruct)(shape, dtype)
            for i, (shape, dtype) in enumerate(outs)
        ]
        seen = {id(a) for a in args}
        extra = [] if self.last is None else [self.last]
        extra += [a for a in self.held.values() if a is not self.last]
        extra = [a for a in extra if id(a) not in seen]
        count, more, results = len(args), len(extra), len(outs)
        hbm = pl.BlockSpec(memory_space=pltpu.HBM)
        specs = [SMEM if i < scalars else hbm if i in fetch or i in raw else VMEM for i in range(count)]
        buffers = []
        for i, (blocks, _) in fetch.items():
            buffers += [pltpu.VMEM(args[i].shape, args[i].dtype), pltpu.SemaphoreType.DMA((blocks,))]
        for i, (blocks, _) in store.items():
            buffers += [pltpu.VMEM(*outs[i]), pltpu.SemaphoreType.DMA((blocks,))]

        def kernel(*refs):
            ins, out = list(refs[:count]), list(refs[count + more : count + more + results])
            rest = list(refs[count + more + results :])
            for i, (_, axis) in fetch.items():
                ins[i] = Fetch(ins[i], rest.pop(0), rest.pop(0), axis)
            for i, (_, axis) in store.items():
                out[i] = Store(out[i], rest.pop(0), rest.pop(0), axis)
            if fetch:
                start_all(*[ins[i] for i in fetch])
            body(*ins, *out, *rest)
            for i in store:
                out[i].finish()

        args = [
            pltpu.with_memory_space_constraint(a, pltpu.HBM) if i in fetch or i in raw else a
            for i, a in enumerate(args)
        ]
        values = pl.pallas_call(
            kernel,
            out_shape=shapes,
            in_specs=specs + [ANY] * more,
            out_specs=[hbm if i in store or i in raw_out else VMEM for i in range(results)],
            scratch_shapes=buffers + list(scratch),
            compiler_params=pltpu.CompilerParams(vmem_limit_bytes=24 * 1024 * 1024),
        )(*args, *extra)
        self.last = values[0]
        return values


def foot_rows(heads):
    return -(-3 * heads // 16) * 16


def put_foot(out, base, totals):
    rows = []
    for total in totals:
        for _ in range(3):
            part = total.astype(BF16)
            rows.append(part.astype(F32))
            total = total - part.astype(F32)
    width = rows[0].shape[1]
    fill = foot_rows(len(totals)) - len(rows)
    if fill:
        rows.append(jnp.zeros((fill, width), F32))
    out[base:, :] = jnp.concatenate(rows, axis=0).astype(BF16)


def get_foot(message, base, heads):
    foot = message[base:, :].astype(F32)
    return [
        foot[3 * h : 3 * h + 1, :] + foot[3 * h + 1 : 3 * h + 2, :] + foot[3 * h + 2 : 3 * h + 3, :]
        for h in range(heads)
    ]


RUN, GROW, TAIL, GROW_BLOCK, TAIL_BLOCK = range(5)


def state_body(keys, values, log_decay, tables, update, packed):
    heads, size = log_decay.buffer.shape[0], tables.shape[2]
    chunks = tables.shape[1] // heads
    width = update.shape[1]
    upper = (
        lax.broadcasted_iota(jnp.int32, (size, size), 0)
        <= lax.broadcasted_iota(jnp.int32, (size, size), 1)
    ).astype(F32)
    pieces = jnp.concatenate(
        [log_decay[:, j * size : (j + 1) * size] for j in range(chunks)], axis=0
    )
    run = lax.dot_general(pieces, upper, NN, precision=HIGH, preferred_element_type=F32)
    ends = [run[j * heads : (j + 1) * heads, size - 1 : size] for j in range(chunks)]
    before, after = [jnp.zeros((heads, 1), F32)], [jnp.zeros((heads, 1), F32)]
    for j in range(chunks - 1):
        before.append(before[-1] + ends[j])
        after.append(after[-1] + ends[chunks - 1 - j])
    before = jnp.concatenate(before, axis=0)
    after = jnp.concatenate(after[::-1], axis=0)
    left = run[:, size - 1 : size] - run
    tables[RUN] = run
    tables[GROW] = jnp.exp(run)
    tables[TAIL] = jnp.exp(left)
    tables[GROW_BLOCK] = jnp.exp(run + before)
    tables[TAIL_BLOCK] = jnp.exp(left + after)
    tail_columns = jnp.exp(left).T
    for h in range(heads):
        cols = slice(h * width, (h + 1) * width)
        state = None
        for j in range(chunks):
            rows = slice(j * size, (j + 1) * size)
            r = j * heads + h
            tail = (keys[rows, cols] * tail_columns[:, r : r + 1]).astype(BF16)
            term = mm(tail, values[rows, cols], TN)
            end = jnp.exp(run[r : r + 1, size - 1 : size])
            state = term if state is None else state * end + term
        update[cols, :] = state
        packed[cols, :] = state.astype(BF16)
    put_foot(packed, heads * width, block_totals(run, heads, width))


def block_totals(run, heads, width):
    chunks, size = run.shape[0] // heads, run.shape[1]
    ends = run[:, size - 1 : size]
    return [
        sum(
            jnp.broadcast_to(ends[j * heads + h : j * heads + h + 1, :], (1, width))
            for j in range(chunks)
        )
        for h in range(heads)
    ]


def combine_body(forward, heads, place, own, packed, other, out, whole):
    core = place[1]
    width = own.shape[1]
    rows = heads * width
    mine, theirs = get_foot(packed, rows, heads), get_foot(other, rows, heads)
    late = core == (1 if forward else 0)
    for h in range(heads):
        at = slice(h * width, (h + 1) * width)
        a, b = own[at, :], other[at, :].astype(F32)
        joined = jnp.where(late, a + jnp.exp(mine[h]) * b, b + jnp.exp(theirs[h]) * a)
        whole[at, :] = joined
    half = rows // 2
    out[:half, :] = whole[pl.ds(pl.multiple_of(core * half, half), half), :].astype(BF16)
    put_foot(out, half, [a + b for a, b in zip(mine, theirs)])


def join_body(forward, heads, chips, place, *refs):
    messages, out = refs[: chips - 1], refs[chips - 1]
    chip, core = place[0], place[1]
    half, width = out.shape
    feet = [get_foot(m, half, heads) for m in messages]
    spans = [jnp.zeros((1, width), F32)] * heads
    head_rows = half * 2 // heads
    groups = max(1, half // head_rows)
    total = [None] * groups
    for k in range(1, chips) if forward else range(chips - 1, 0, -1):
        used = (k <= chip) if forward else (k > chip)
        for g in range(groups):
            span = spans[0] if heads == 1 else jnp.where(core == 0, spans[g], spans[groups + g])
            factor = jnp.where(used, jnp.exp(span), 0.0)
            at = slice(g * half // groups, (g + 1) * half // groups)
            term = factor * messages[k - 1][at, :].astype(F32)
            total[g] = term if total[g] is None else total[g] + term
        spans = [span + foot for span, foot in zip(spans, feet[k - 1])]
    for g in range(groups):
        out[g * half // groups : (g + 1) * half // groups, :] = total[g].astype(BF16)


def enter(forward, heads, place, mine, theirs, other, out):
    core = place[1]
    half, width = mine.shape
    rows = 2 * half
    out[pl.ds(pl.multiple_of(core * half, half), half), :] = mine[...].astype(F32)
    out[pl.ds(pl.multiple_of((1 - core) * half, half), half), :] = theirs[...].astype(F32)
    totals = get_foot(other, rows, heads)
    late = core == (1 if forward else 0)
    for h in range(heads):
        at = slice(h * width, (h + 1) * width)
        now = out[at, :]
        moved = other[at, :].astype(F32) + jnp.exp(totals[h]) * now
        out[at, :] = jnp.where(late, moved, now)


def causal_mask(size):
    return lax.broadcasted_iota(jnp.int32, (size, size), 0) >= lax.broadcasted_iota(
        jnp.int32, (size, size), 1
    )


def decay_of(run, columns, r, causal):
    return jnp.exp(jnp.where(causal, columns[:, r : r + 1] - run[r : r + 1, :], -jnp.inf))


def local_body(queries, keys, values, tables, mixed, grown_rows):
    size = tables.shape[2]
    length, columns = mixed.shape
    chunks = length // size
    heads = tables.shape[1] // chunks
    width = columns // heads
    causal = causal_mask(size)
    run = tables[RUN]
    sums, grow, tails = run.T, tables[GROW].T, tables[TAIL].T
    for h in range(heads):
        cols = slice(h * width, (h + 1) * width)
        state = None
        for j in range(chunks):
            rows = slice(j * size, (j + 1) * size)
            r = j * heads + h
            query, key, value = queries[rows, cols], keys[rows, cols], values[rows, cols]
            weight = (mm(query, key, NT) * decay_of(run, sums, r, causal)).astype(BF16)
            grown = query * grow[:, r : r + 1]
            grown_rows[cols, rows] = grown.T.astype(BF16)
            out = mm(weight, value, NN)
            if state is not None:
                out = out + mm(grown.astype(BF16), state.astype(BF16), NN)
            mixed[rows, cols] = out
            if j < chunks - 1:
                term = mm((key * tails[:, r : r + 1]).astype(BF16), value, TN)
                end = grow[size - 1 : size, r : r + 1]
                state = term if state is None else state * end + term
        grown_rows.send(h)


def norm_body(
    heads, place, mixed, queries, tables, mine, theirs, other, attended, inverse, incoming
):
    width = mine.shape[1]
    size = tables.shape[2]
    chunks = tables.shape[1] // heads
    enter(True, heads, place, mine, theirs, other, incoming)
    grow = tables[GROW_BLOCK].T
    ones = jnp.full((width, width), 1.0 / width, BF16)
    lane = lax.broadcasted_iota(jnp.int32, (size, width), 1)
    low = [incoming[h * width : (h + 1) * width, :].astype(BF16) for h in range(heads)]
    for j in range(chunks):
        rows = slice(j * size, (j + 1) * size)
        scales = jnp.zeros((size, width), F32)
        for h in range(heads):
            cols = slice(h * width, (h + 1) * width)
            r = j * heads + h
            grown = (queries[rows, cols] * grow[:, r : r + 1]).astype(BF16)
            total = mixed[rows, cols] + mm(grown, low[h], NN)
            scale = lax.rsqrt(mm((total * total).astype(BF16), ones, NN) + 1e-05)
            scales = jnp.where(lane == h, scale, scales)
            attended[rows, cols] = (total * scale).astype(BF16)
        inverse[j * heads : (j + 1) * heads, :] = scales.T[:heads, :]
        attended.send(j)


def head_grad_body(size, starts, weight, whole, out):
    for t in range(out.shape[0] // size):
        rows = slice(t * size, (t + 1) * size)
        out[rows, :] = mm(whole[rows, :], weight[...], NN)


def early_body(size, place, starts, weight, attended, *refs):
    pieces, mine, theirs, out, rows_of_weight, semaphores = (
        refs[:3], refs[3], refs[4:7], refs[7], refs[8], refs[9]
    )
    core = place[1]
    part = mine.shape[1]
    copies = []
    for i in range(3):
        start = pl.multiple_of(starts[i] * 64, 64)
        copies.append(
            pltpu.make_async_copy(
                weight.at[pl.ds(start, 2 * part), :], rows_of_weight.at[i], semaphores.at[i]
            )
        )
        copies[i].start()
    for i, piece in enumerate(pieces):
        product = mm(piece[...], attended[...], TN)
        low, high = product[:part, :].astype(BF16), product[part:, :].astype(BF16)
        mine[i] = jnp.where(core == 0, low, high)
        theirs[i][...] = jnp.where(core == 0, high, low)
    for copy in copies:
        copy.wait()
    for t in range(out.shape[0] // size):
        rows = slice(t * size, (t + 1) * size)
        out[rows, :] = sum(mm(piece[rows, :], rows_of_weight[i], NN) for i, piece in enumerate(pieces))


def late_body(heads, number, place, starts, weight, attended, *refs):
    pieces = refs[:number]
    refs = refs[number:]
    partial, inverse, grown_rows, tables, mixed_grad, update, packed = refs[:7]
    width = update.shape[1]
    size = tables.shape[2]
    chunks = tables.shape[1] // heads
    if number:
        mine, theirs, rows_of_weight, semaphores = refs[7:]
        core = place[1]
        part = mine.shape[0]
        start = pl.multiple_of(starts[0] * 64, 64)
        copy = pltpu.make_async_copy(
            weight.at[pl.ds(start, 2 * part), :], rows_of_weight, semaphores.at[0]
        )
        copy.start()
        low, high = [mm(p[...], attended[...], TN).astype(BF16) for p in pieces]
        mine[...] = jnp.where(core == 0, low, high)
        theirs[...] = jnp.where(core == 0, high, low)
        copy.wait()
    ones = jnp.full((width, width), 1.0 / width, BF16)
    states = [None] * heads
    run = tables[RUN]
    scales = inverse[...].T
    for j in reversed(range(chunks)):
        rows = slice(j * size, (j + 1) * size)
        total = partial[rows, :]
        for i, piece in enumerate(pieces):
            total = total + mm(
                piece[rows, :], rows_of_weight[i * part : (i + 1) * part, :], NN
            )
        for h in range(heads):
            cols = slice(h * width, (h + 1) * width)
            r = j * heads + h
            grad = total[:, cols]
            unit = attended[rows, cols].astype(F32)
            mean = mm((grad * unit).astype(BF16), ones, NN)
            grad = ((grad - unit * mean) * scales[:, r : r + 1]).astype(BF16)
            mixed_grad[rows, cols] = grad
            term = mm(grown_rows[cols, rows], grad, NN)
            end = jnp.exp(run[r : r + 1, size - 1 : size])
            states[h] = term if states[h] is None else term + states[h] * end
    for h in range(heads):
        at = slice(h * width, (h + 1) * width)
        update[at, :] = states[h]
        packed[at, :] = states[h].astype(BF16)
    put_foot(packed, heads * width, block_totals(run, heads, width))


def back_body(
    heads, queries, keys, values, mixed_grad, tables, incoming, grown_rows,
    query_grad, key_grad, value_grad, states,
):
    width = incoming.shape[1]
    size = tables.shape[2]
    chunks = tables.shape[1] // heads
    causal = causal_mask(size)
    run = tables[RUN]
    sums, grow, tails = run.T, tables[GROW].T, tables[TAIL].T
    for h in range(heads):
        cols = slice(h * width, (h + 1) * width)
        state = incoming[cols, :]
        for j in range(chunks):
            rows = slice(j * size, (j + 1) * size)
            r = j * heads + h
            states[j] = state.astype(BF16)
            if j < chunks - 1:
                tail = (keys[rows, cols] * tails[:, r : r + 1]).astype(BF16)
                state = state * grow[size - 1 : size, r : r + 1] + mm(tail, values[rows, cols], TN)
        back = None
        for j in reversed(range(chunks)):
            rows = slice(j * size, (j + 1) * size)
            r = j * heads + h
            grad, query = mixed_grad[rows, cols], queries[rows, cols]
            key, value = keys[rows, cols], values[rows, cols]
            decay = decay_of(run, sums, r, causal)
            weight = (mm(query, key, NT) * decay).astype(BF16)
            masked = (mm(grad, value, NT) * decay).astype(BF16)
            grown = (grad * grow[:, r : r + 1]).astype(BF16)
            query_grad[rows, cols] = (mm(masked, key, NN) + mm(grown, states[j], NT)).astype(BF16)
            key_part = mm(masked, query, TN)
            value_part = mm(weight, grad, TN)
            term = mm(grown_rows[cols, rows], grad, NN)
            if back is not None:
                tail = tails[:, r : r + 1]
                low = back.astype(BF16)
                key_part = key_part + mm((value * tail).astype(BF16), low, NT)
                value_part = value_part + mm((key * tail).astype(BF16), low, NN)
                term = term + back * grow[size - 1 : size, r : r + 1]
            back = term
            key_grad[rows, cols] = key_part.astype(BF16)
            value_grad[rows, cols] = value_part.astype(BF16)
        query_grad.send(h)
        key_grad.send(h)
        value_grad.send(h)


def final_body(
    heads, place, keys, values, tables, mine, theirs, other, key_part, value_part,
    key_grad, value_grad, outgoing,
):
    width = mine.shape[1]
    size = tables.shape[2]
    chunks = tables.shape[1] // heads
    enter(False, heads, place, mine, theirs, other, outgoing)
    tails = tables[TAIL_BLOCK].T
    for h in range(heads):
        cols = slice(h * width, (h + 1) * width)
        state = outgoing[cols, :].astype(BF16)
        for j in range(chunks):
            rows = slice(j * size, (j + 1) * size)
            r = j * heads + h
            tail = tails[:, r : r + 1]
            key_grad[rows, cols] = (
                key_part[rows, cols] + mm((values[rows, cols] * tail).astype(BF16), state, NT)
            ).astype(BF16)
            value_grad[rows, cols] = (
                value_part[rows, cols] + mm((keys[rows, cols] * tail).astype(BF16), state, NN)
            ).astype(BF16)
        key_grad.send(h)
        value_grad.send(h)


def fold_body(place, mine, low, middle, high, kept, sent):
    odd = place[2] % 2 == 1
    sums = [mine[i].astype(F32) + part[...].astype(F32) for i, part in enumerate((low, middle, high))]
    kept[0] = jnp.where(odd, sums[1], sums[0]).astype(BF16)
    kept[1] = sums[2].astype(BF16)
    sent[0] = jnp.where(odd, sums[0], sums[1]).astype(BF16)
    sent[1] = sums[2].astype(BF16)


def fold_again_body(place, kept, arrived, total, sent):
    turn = place[2]
    first = kept[0].astype(F32) + arrived[0].astype(F32)
    second = kept[1].astype(F32) + arrived[1].astype(F32)
    total[...] = jnp.where(turn == 2, second, first)
    sent[...] = jnp.where(turn == 0, second, first).astype(BF16)


def fold_last_body(mine, arrived, kept, sent):
    value = mine[...].astype(F32) + arrived[...].astype(F32)
    kept[...] = value
    sent[...] = value.astype(BF16)


def add_body(kept, arrived, total, sent):
    value = kept[...] + arrived[...].astype(F32)
    total[...] = value
    sent[...] = value.astype(BF16)


def cut_body(part, x, y, low, high, *rest):
    buffers, semaphores = rest[:2], rest[2]
    loads = [
        pltpu.make_async_copy(source, buffer, semaphores.at[i])
        for i, (source, buffer) in enumerate(
            ((x.at[:, :part], buffers[0]), (y.at[:, part:], buffers[1]))
        )
    ]
    stores = [
        pltpu.make_async_copy(buffer, target, semaphores.at[2 + i])
        for i, (buffer, target) in enumerate(((buffers[0], low), (buffers[1], high)))
    ]
    for load in loads:
        load.start()
    for load, store in zip(loads, stores):
        load.wait()
        store.start()
    for store in stores:
        store.wait()


def hop(value, step, senders, chips, count):
    moves = [
        (s * count + y, ((s // 2 ^ step) * 2 + s % 2) * count + y)
        for s in range(2 * chips)
        for y in range(count)
        if s // 2 ^ y in senders
    ]
    return lax.ppermute(value, ("seq", "head"), moves)


class Chain:
    def __init__(self, line, forward, heads, chips, place, update, packed):
        self.line, self.forward, self.heads, self.chips = line, forward, heads, chips
        self.place, self.update, self.packed = place, update, packed
        self.other = self.swap(packed)

    def swap(self, value):
        return lax.ppermute(value, "seq", [(i, i ^ 1) for i in range(2 * self.chips)])

    def send(self):
        rows, width = self.update.shape
        self.half = (rows // 2, width)
        message, = self.line.call(
            functools.partial(combine_body, self.forward, self.heads),
            [((rows // 2 + foot_rows(self.heads), width), BF16)],
            self.place, self.update, self.packed, self.other,
            scratch=[pltpu.VMEM((rows, width), F32)], scalars=1,
        )
        self.line.held[self] = self.other
        self.arrived = [
            lax.ppermute(
                message, "seq",
                [(i, (i // 2 + k) % self.chips * 2 + i % 2) for i in range(2 * self.chips)],
            )
            for k in range(1, self.chips)
        ]

    def join(self):
        self.mine, = self.line.call(
            functools.partial(join_body, self.forward, self.heads, self.chips),
            [(self.half, BF16)], self.place, *self.arrived, scalars=1,
        )
        self.theirs = self.swap(self.mine)

    def done(self):
        self.line.held.pop(self)
        return self.mine, self.theirs, self.other


def on_device(seq_size, head_size, queries, keys, values, log_decay, out_weight, out_grad):
    length, columns = queries.shape
    heads = log_decay.shape[0]
    width = columns // heads
    size = 256 if length % 256 == 0 else length
    chunks = length // size
    chips = seq_size // 2
    near = head_size == 4 and chips == 4
    seq, head = lax.axis_index("seq"), lax.axis_index("head")
    place = jnp.stack([seq // 2, seq % 2, (seq // 2) ^ head]).astype(jnp.int32)
    block = out_grad.shape[1]
    part = block // 2
    move = lambda a, k: lax.ppermute(a, "head", [(i, i ^ k) for i in range(head_size)])
    if near:
        x, y = move(out_grad, 1), move(out_grad, 2)
    else:
        whole = lax.all_gather(out_grad, "head", axis=1, tiled=True)
    state = ((heads * width, width), F32)
    message = ((heads * width + foot_rows(heads), width), BF16)
    rows = (length, columns)
    line = Line()
    held = line.held

    def starts_of(group):
        return jnp.stack(
            [((head ^ k) * block + side * part) // 64 for k, side in group]
        ).astype(jnp.int32)

    tables, update, packed = line.call(
        state_body, [((5, chunks * heads, size), F32), state, message], keys, values, log_decay,
        fetch={2: 1, 0: heads, 1: heads},
    )
    forward = Chain(line, True, heads, chips, place, update, packed)
    pass
    forward.send()
    mixed, grown_rows = line.call(
        local_body, [(rows, F32), ((columns, length), BF16)], queries, keys, values, tables,
        fetch={i: heads for i in range(3)}, store={1: (heads, 0)},
    )
    held.update(mixed=mixed)
    forward.join()
    entering = forward.done()
    held.pop("mixed")
    attended, inverse, incoming = line.call(
        functools.partial(norm_body, heads),
        [(rows, BF16), ((chunks * heads, size), F32), state],
        place, mixed, queries, tables, *entering, scalars=1,
        fetch={2: (chunks, 0)}, store={0: (chunks, 0)},
    )
    held.update(inverse=inverse, incoming=incoming)
    swap = lambda a: lax.ppermute(a, "seq", [(i, i ^ 1) for i in range(2 * chips)])
    shape = (part, columns)
    if near:
        low, high = line.call(
            functools.partial(cut_body, part), [((length, part), BF16)] * 2, x, y,
            scratch=[pltpu.VMEM((length, part), BF16)] * 2 + [pltpu.SemaphoreType.DMA((4,))],
            raw=(0, 1), raw_out=(0, 1),
        )
        diagonal = [move(low, 2), move(high, 1)]
        products, *theirs, partial = line.call(
            functools.partial(early_body, size),
            [((3,) + shape, BF16)] + [(shape, BF16)] * 3 + [(rows, F32)],
            place, starts_of([(0, 0), (1, 0), (2, 0)]), out_weight, attended, out_grad, x, y,
            scratch=[pltpu.VMEM((3, block, columns), BF16), pltpu.SemaphoreType.DMA((3,))],
            scalars=2, raw=(2,), fetch={3: 1, 4: 1, 5: 1, 6: 1},
        )
        arrived = [swap(a) for a in theirs]
        held["partial"] = partial
        kept, sent = line.call(
            fold_body, [((2,) + shape, BF16), ((2,) + shape, BF16)],
            place, products, *arrived, scalars=1,
        )
        arrived = hop(sent, 1, (0, 1, 2, 3), chips, head_size)
        held["kept"] = kept
        held.pop("partial")
        mixed_grad, back_update, back_packed, last, theirs = line.call(
            functools.partial(late_body, heads, 2),
            [(rows, BF16), state, message, (shape, BF16), (shape, BF16)],
            place, starts_of([(3, 0)]), out_weight, attended, *diagonal, partial, inverse,
            grown_rows, tables,
            scratch=[pltpu.VMEM((block, columns), BF16), pltpu.SemaphoreType.DMA((1,))],
            scalars=2, raw=(2,), fetch={3: 1, 4: 1, 5: 1, 8: (1, 0)},
        )
        held["last"] = last
        last_arrived = swap(theirs)
    else:
        partial, = line.call(
            functools.partial(head_grad_body, size), [(rows, F32)],
            jnp.zeros((1,), jnp.int32), out_weight, whole, scalars=1,
        )
        mixed_grad, back_update, back_packed = line.call(
            functools.partial(late_body, heads, 0), [(rows, BF16), state, message],
            place, jnp.zeros((1,), jnp.int32), out_weight, attended, partial, inverse,
            grown_rows, tables, scalars=2,
        )
    back = Chain(line, False, heads, chips, place, back_update, back_packed)
    held.pop("inverse")
    held["mixed_grad"] = mixed_grad
    held["update"] = back_update
    if near:
        held.pop("last")
        last, sent = line.call(
            fold_last_body, [(shape, F32), (shape, BF16)], last, last_arrived
        )
        held["last"] = last
        last_arrived = hop(sent, 1, (0, 2), chips, head_size)
    held.pop("update")
    back.send()
    if near:
        held.pop("kept")
        kept, sent = line.call(
            fold_again_body, [(shape, F32), (shape, BF16)], place, kept, arrived, scalars=1
        )
        arrived = hop(sent, 2, (0, 2, 3), chips, head_size)
    query_grad, key_part, value_part = line.call(
        functools.partial(back_body, heads), [(rows, BF16), (rows, BF16), (rows, BF16)],
        queries, keys, values, mixed_grad, tables, incoming, grown_rows,
        fetch={0: heads, 1: heads, 2: heads, 6: (heads, 0)}, store={i: heads for i in range(3)},
        scratch=[pltpu.VMEM((chunks, width, width), BF16)],
    )
    for name in ("mixed_grad", "incoming"):
        held.pop(name)
    back.join()
    if near:
        held.pop("last")
        last, sent = line.call(add_body, [(shape, F32), (shape, BF16)], last, last_arrived)
        last_arrived = hop(sent, 2, (1,), chips, head_size)
    key_grad, value_grad = line.call(
        functools.partial(final_body, heads), [(rows, BF16)] * 2,
        place, keys, values, tables, *back.done(), key_part, value_part,
        scratch=[pltpu.VMEM((heads * width, width), F32)], scalars=1,
        fetch={1: heads, 2: heads, 7: heads, 8: heads}, store={0: heads, 1: heads},
    )
    if near:
        weight_grad = jnp.where(
            place[2] == 3, last + last_arrived.astype(F32), kept + arrived.astype(F32)
        )
    else:
        weight_grad = lax.psum_scatter(
            mm(whole, attended, TN), "seq", scatter_dimension=0, tiled=True
        )
    return attended, query_grad, key_grad, value_grad, weight_grad.astype(BF16)


def solution(mesh):
    block = P("seq", "head")
    return jax.shard_map(
        functools.partial(on_device, mesh.shape["seq"], mesh.shape["head"]),
        mesh=mesh,
        in_specs=(block, block, block, P("head", "seq"), P(None, "head"), block),
        out_specs=(block,) * 5,
        check_vma=False,
    )
```

```python
import functools

import jax
import jax.numpy as jnp
from jax import lax
from jax.experimental import pallas as pl
from jax.experimental.pallas import tpu as pltpu
from jax.sharding import PartitionSpec as P

HIGH = lax.Precision.HIGHEST
F32 = jnp.float32
BF16 = jnp.bfloat16
VMEM = pl.BlockSpec(memory_space=pltpu.VMEM)
ANY = pl.BlockSpec(memory_space=pl.ANY)
NN = (((1,), (0,)), ((), ()))
NT = (((1,), (1,)), ((), ()))
TN = (((0,), (0,)), ((), ()))


def mm(left, right, dims):
    return lax.dot_general(left, right, dims, preferred_element_type=F32)


class Fetch:
    def __init__(self, source, buffer, semaphores, axis=1):
        self.buffer, self.axis = buffer, axis
        self.count = semaphores.shape[0]
        self.step = buffer.shape[axis] // self.count
        at = [
            (slice(None),) * axis + (slice(i * self.step, (i + 1) * self.step),)
            for i in range(self.count)
        ]
        self.copies = [
            pltpu.make_async_copy(source.at[p], buffer.at[p], semaphores.at[i])
            for i, p in enumerate(at)
        ]
        self.waiting = set(range(self.count))

        self.shape = buffer.shape

    def __getitem__(self, index):
        span = index[self.axis] if isinstance(index, tuple) else slice(None)
        first, last = span.start or 0, span.stop or self.buffer.shape[self.axis]
        wanted = {i for i in self.waiting if first < (i + 1) * self.step and i * self.step < last}
        if wanted and 0 not in self.waiting or len(wanted) > 1:
            wanted = set(self.waiting)
        for i in sorted(wanted):
            self.copies[i].wait()
        self.waiting -= wanted
        return self.buffer[index]


def start_all(*fetches):
    for i in range(max(f.count for f in fetches)):
        for f in fetches:
            if i < f.count:
                f.copies[i].start()


class Store(Fetch):
    def __init__(self, target, buffer, semaphores, axis=1):
        self.buffer, self.axis = buffer, axis
        self.count = semaphores.shape[0]
        self.step = buffer.shape[axis] // self.count
        at = [
            (slice(None),) * axis + (slice(i * self.step, (i + 1) * self.step),)
            for i in range(self.count)
        ]
        self.copies = [
            pltpu.make_async_copy(buffer.at[p], target.at[p], semaphores.at[i])
            for i, p in enumerate(at)
        ]

        self.shape, self.ready, self.left = buffer.shape, [], set(range(self.count))

    def __setitem__(self, index, value):
        self.buffer[index] = value

    def send(self, i):
        self.ready.append(i)
        if len(self.ready) * 2 >= self.count:
            self.start(self.ready)
            self.ready = []

    def start(self, blocks):
        for i in blocks:
            self.copies[i].start()
            self.left.remove(i)

    def finish(self):
        self.start(sorted(self.left))
        for copy in self.copies:
            copy.wait()


GROUP = 4


def together(steps):
    steps = list(steps)
    for i in range(0, len(steps), GROUP):
        running = steps[i : i + GROUP]
        while running:
            running = [step for step in running if next(step, None) is not None]


def here():
    seq, head = lax.axis_index("seq"), lax.axis_index("head")
    return seq >> 1, seq & 1, (seq >> 1) ^ head, head


class Line:
    def __init__(self):
        self.last = None
        self.held = {}

    def call(self, body, outs, *args, scratch=(), place=False, fetch={}, store={}, raw=(), raw_out=(), loose=()):
        fetch = {i: f if isinstance(f, tuple) else (f, 1) for i, f in fetch.items()}
        store = {i: f if isinstance(f, tuple) else (f, 1) for i, f in store.items()}
        shapes = [
            (pltpu.HBM if i in store or i in raw_out else jax.ShapeDtypeStruct)(shape, dtype)
            for i, (shape, dtype) in enumerate(outs)
        ]
        seen = {id(a) for a in args}
        extra = [] if self.last is None else [self.last]
        extra += [a for a in self.held.values()]
        extra = [a for a in extra if id(a) not in seen]
        count, more, results = len(args), len(extra), len(outs)
        hbm = pl.BlockSpec(memory_space=pltpu.HBM)
        specs = [ANY if i in loose else hbm if i in fetch else hbm if i in raw else VMEM for i in range(count)]
        buffers = []
        for i, (blocks, _) in fetch.items():
            buffers += [pltpu.VMEM(args[i].shape, args[i].dtype), pltpu.SemaphoreType.DMA((blocks,))]
        for i, (blocks, _) in store.items():
            buffers += [pltpu.VMEM(*outs[i]), pltpu.SemaphoreType.DMA((blocks,))]

        def kernel(*refs):
            ins, out = list(refs[:count]), list(refs[count + more : count + more + results])
            rest = list(refs[count + more + results :])
            for i, (_, axis) in fetch.items():
                ins[i] = Fetch(ins[i], rest.pop(0), rest.pop(0), axis)
            for i, (_, axis) in store.items():
                out[i] = Store(out[i], rest.pop(0), rest.pop(0), axis)
            if fetch:
                start_all(*[ins[i] for i in fetch])
            if place:
                ins = [here()] + ins
            body(*ins, *out, *rest)
            for i in store:
                out[i].finish()

        args = [
            pltpu.with_memory_space_constraint(a, pltpu.HBM) if (i in fetch or i in raw) and i not in loose else a
            for i, a in enumerate(args)
        ]
        values = pl.pallas_call(
            kernel,
            out_shape=shapes,
            in_specs=specs + [ANY] * more,
            out_specs=[hbm if i in store or i in raw_out else VMEM for i in range(results)],
            scratch_shapes=buffers + list(scratch),
            compiler_params=pltpu.CompilerParams(vmem_limit_bytes=24 * 1024 * 1024),
        )(*args, *extra)
        least = min(range(results), key=lambda i: values[i].size * values[i].dtype.itemsize)
        self.last = values[least]
        if least in store or least in raw_out:
            self.last = pltpu.with_memory_space_constraint(self.last, pltpu.HBM)
        return values


def foot_rows(heads):
    return -(-3 * heads // 16) * 16


def put_foot(out, base, totals):
    rows = []
    for total in totals:
        for _ in range(3):
            part = total.astype(BF16)
            rows.append(part.astype(F32))
            total = total - part.astype(F32)
    width = rows[0].shape[1]
    fill = foot_rows(len(totals)) - len(rows)
    if fill:
        rows.append(jnp.zeros((fill, width), F32))
    out[base:, :] = jnp.concatenate(rows, axis=0).astype(BF16)


def get_foot(message, base, heads):
    foot = message[base:, :].astype(F32)
    return [
        foot[3 * h : 3 * h + 1, :] + foot[3 * h + 1 : 3 * h + 2, :] + foot[3 * h + 2 : 3 * h + 3, :]
        for h in range(heads)
    ]


RUN, GROW, TAIL, GROW_BLOCK, TAIL_BLOCK = range(5)


def state_body(keys, values, log_decay, tables, update, packed, states):
    heads, size = log_decay.buffer.shape[0], tables.shape[2]
    chunks = tables.shape[1] // heads
    width = update.shape[1]
    upper = (
        lax.broadcasted_iota(jnp.int32, (size, size), 0)
        <= lax.broadcasted_iota(jnp.int32, (size, size), 1)
    ).astype(F32)
    pieces = jnp.concatenate(
        [log_decay[:, j * size : (j + 1) * size] for j in range(chunks)], axis=0
    )
    run = lax.dot_general(pieces, upper, NN, precision=HIGH, preferred_element_type=F32)
    ends = [run[j * heads : (j + 1) * heads, size - 1 : size] for j in range(chunks)]
    before, after = [jnp.zeros((heads, 1), F32)], [jnp.zeros((heads, 1), F32)]
    for j in range(chunks - 1):
        before.append(before[-1] + ends[j])
        after.append(after[-1] + ends[chunks - 1 - j])
    before = jnp.concatenate(before, axis=0)
    after = jnp.concatenate(after[::-1], axis=0)
    left = run[:, size - 1 : size] - run
    tables[RUN] = run
    tables[GROW] = jnp.exp(run)
    tables[TAIL] = jnp.exp(left)
    tables[GROW_BLOCK] = jnp.exp(run + before)
    tables[TAIL_BLOCK] = jnp.exp(left + after)
    tail_columns = jnp.exp(left).T
    def product(h, j, terms):
        cols, rows = slice(h * width, (h + 1) * width), slice(j * size, (j + 1) * size)
        r = j * heads + h
        tail = (keys[rows, cols] * tail_columns[:, r : r + 1]).astype(BF16)
        value = values[rows, cols]
        yield True
        terms.append(mm(tail, value, TN))
        yield True

    for h in range(heads):
        cols = slice(h * width, (h + 1) * width)
        terms = []
        together(product(h, j, terms) for j in range(chunks))
        state = None
        for j in range(chunks):
            r = j * heads + h
            at = slice((h * chunks + j) * width, (h * chunks + j + 1) * width)
            states[at, :] = jnp.zeros((width, width), BF16) if j == 0 else state.astype(BF16)
            end = jnp.exp(run[r : r + 1, size - 1 : size])
            state = terms[j] if state is None else state * end + terms[j]
        states.send(h)
        update[cols, :] = state
        packed[cols, :] = state.astype(BF16)
    put_foot(packed, heads * width, block_totals(run, heads, width))


def block_totals(run, heads, width):
    chunks, size = run.shape[0] // heads, run.shape[1]
    ends = run[:, size - 1 : size]
    return [
        sum(
            jnp.broadcast_to(ends[j * heads + h : j * heads + h + 1, :], (1, width))
            for j in range(chunks)
        )
        for h in range(heads)
    ]


def combine_body(forward, heads, place, own, packed, other, out, whole):
    core = place[1]
    width = own.shape[1]
    rows = heads * width
    mine, theirs = get_foot(packed, rows, heads), get_foot(other, rows, heads)
    late = core == (1 if forward else 0)
    for h in range(heads):
        at = slice(h * width, (h + 1) * width)
        a, b = own[at, :], other[at, :].astype(F32)
        joined = jnp.where(late, a + jnp.exp(mine[h]) * b, b + jnp.exp(theirs[h]) * a)
        whole[at, :] = joined
    half = rows // 2
    out[:half, :] = whole[pl.ds(pl.multiple_of(core * half, half), half), :].astype(BF16)
    put_foot(out, half, [a + b for a, b in zip(mine, theirs)])


def join_body(forward, heads, chips, place, *refs):
    messages, out = refs[: chips - 1], refs[chips - 1]
    chip, core = place[0], place[1]
    half, width = out.shape
    feet = [get_foot(m, half, heads) for m in messages]
    spans = [jnp.zeros((1, width), F32)] * heads
    head_rows = half * 2 // heads
    groups = max(1, half // head_rows)
    total = [None] * groups
    for k in range(1, chips) if forward else range(chips - 1, 0, -1):
        used = (k <= chip) if forward else (k > chip)
        for g in range(groups):
            span = spans[0] if heads == 1 else jnp.where(core == 0, spans[g], spans[groups + g])
            factor = jnp.where(used, jnp.exp(span), 0.0)
            at = slice(g * half // groups, (g + 1) * half // groups)
            term = factor * messages[k - 1][at, :].astype(F32)
            total[g] = term if total[g] is None else total[g] + term
        spans = [span + foot for span, foot in zip(spans, feet[k - 1])]
    for g in range(groups):
        out[g * half // groups : (g + 1) * half // groups, :] = total[g].astype(BF16)


def enter(forward, heads, place, mine, theirs, other, out):
    core = place[1]
    half, width = mine.shape
    rows = 2 * half
    out[pl.ds(pl.multiple_of(core * half, half), half), :] = mine[...].astype(F32)
    out[pl.ds(pl.multiple_of((1 - core) * half, half), half), :] = theirs[...].astype(F32)
    totals = get_foot(other, rows, heads)
    late = core == (1 if forward else 0)
    for h in range(heads):
        at = slice(h * width, (h + 1) * width)
        now = out[at, :]
        moved = other[at, :].astype(F32) + jnp.exp(totals[h]) * now
        out[at, :] = jnp.where(late, moved, now)


def causal_mask(size):
    return lax.broadcasted_iota(jnp.int32, (size, size), 0) >= lax.broadcasted_iota(
        jnp.int32, (size, size), 1
    )


def decay_of(run, columns, r, causal):
    return jnp.exp(jnp.where(causal, columns[:, r : r + 1] - run[r : r + 1, :], -jnp.inf))


def local_body(queries, keys, values, tables, states, mixed, grown_rows):
    size = tables.shape[2]
    length, columns = mixed.shape
    chunks = length // size
    heads = tables.shape[1] // chunks
    width = columns // heads
    causal = causal_mask(size)
    run = tables[RUN]
    sums, grow = run.T, tables[GROW].T
    def step(h, j):
        cols, rows = slice(h * width, (h + 1) * width), slice(j * size, (j + 1) * size)
        r = j * heads + h
        query, key, value = queries[rows, cols], keys[rows, cols], values[rows, cols]
        scores = mm(query, key, NT)
        grown = (query * grow[:, r : r + 1]).astype(BF16)
        yield True
        weight = (scores * decay_of(run, sums, r, causal)).astype(BF16)
        turned = grown.T
        yield True
        out = mm(weight, value, NN)
        if j:
            at = slice((h * chunks + j) * width, (h * chunks + j + 1) * width)
            out = out + mm(grown, states[at, :], NN)
        yield True
        grown_rows[cols, rows] = turned
        mixed[rows, cols] = out
        yield True

    for h in range(heads):
        together(step(h, j) for j in range(chunks))
        grown_rows.send(h)


def norm_body(
    heads, place, mixed, queries, tables, mine, theirs, other, attended, inverse, incoming
):
    width = mine.shape[1]
    size = tables.shape[2]
    chunks = tables.shape[1] // heads
    enter(True, heads, place, mine, theirs, other, incoming)
    grow = tables[GROW_BLOCK].T
    ones = jnp.full((width, width), 1.0 / width, BF16)
    lane = lax.broadcasted_iota(jnp.int32, (size, width), 1)
    low = [incoming[h * width : (h + 1) * width, :].astype(BF16) for h in range(heads)]
    def step(j, h, scales):
        cols, rows = slice(h * width, (h + 1) * width), slice(j * size, (j + 1) * size)
        r = j * heads + h
        grown = (queries[rows, cols] * grow[:, r : r + 1]).astype(BF16)
        yield True
        total = mixed[rows, cols] + mm(grown, low[h], NN)
        square = (total * total).astype(BF16)
        yield True
        scale = lax.rsqrt(mm(square, ones, NN) + 1e-05)
        yield True
        scales[0] = jnp.where(lane == h, scale, scales[0])
        attended[rows, cols] = (total * scale).astype(BF16)
        yield True

    for j in range(chunks):
        scales = [jnp.zeros((size, width), F32)]
        together(step(j, h, scales) for h in range(heads))
        inverse[j * heads : (j + 1) * heads, :] = scales[0].T[:heads, :]
        attended.send(j)


def head_grad_body(size, weight, whole, out):
    for t in range(out.shape[0] // size):
        rows = slice(t * size, (t + 1) * size)
        out[rows, :] = mm(whole[rows, :], weight[...], NN)


def weight_copies(head, blocks, weight, rows_of_weight, semaphores):
    depth = rows_of_weight.shape[0] // len(blocks)
    return [
        pltpu.make_async_copy(
            weight.at[pl.ds(pl.multiple_of((head ^ k) * depth, depth), depth), :],
            rows_of_weight.at[i * depth : (i + 1) * depth, :],
            semaphores.at[i],
        )
        for i, k in enumerate(blocks)
    ]


def early_body(size, place, weight, attended, *refs):
    pieces, mine, theirs, out, rows_of_weight, semaphores = (
        refs[:3], refs[3], refs[4:7], refs[7], refs[8], refs[9]
    )
    _, core, _, head = place
    part = mine.shape[1]
    copies = weight_copies(head, (0, 1, 2), weight, rows_of_weight, semaphores)
    for copy in copies:
        copy.start()
    for i, piece in enumerate(pieces):
        product = mm(piece[...], attended[...], TN)
        low, high = product[:part, :].astype(BF16), product[part:, :].astype(BF16)
        mine[i] = jnp.where(core == 0, low, high)
        theirs[i][...] = jnp.where(core == 0, high, low)
    for copy in copies:
        copy.wait()
    for t in range(out.shape[0] // size):
        rows = slice(t * size, (t + 1) * size)
        out[rows, :] = sum(
            mm(piece[rows, :], rows_of_weight[2 * part * i : 2 * part * (i + 1), :], NN)
            for i, piece in enumerate(pieces)
        )


def late_body(heads, number, place, weight, attended, *refs):
    pieces = refs[:number]
    refs = refs[number:]
    partial, inverse, grown_rows, tables, mixed_grad, update, packed, exits = refs[:8]
    width = update.shape[1]
    size = tables.shape[2]
    chunks = tables.shape[1] // heads
    if number:
        mine, theirs, rows_of_weight, semaphores = refs[8:]
        _, core, _, head = place
        part = mine.shape[0]
        copy, = weight_copies(head, (3,), weight, rows_of_weight, semaphores)
        copy.start()
        low, high = [mm(p[...], attended[...], TN).astype(BF16) for p in pieces]
        mine[...] = jnp.where(core == 0, low, high)
        theirs[...] = jnp.where(core == 0, high, low)
        copy.wait()
    ones = jnp.full((width, width), 1.0 / width, BF16)
    states = [None] * heads
    run = tables[RUN]
    scales = inverse[...].T

    def step(j, h, total):
        cols, rows = slice(h * width, (h + 1) * width), slice(j * size, (j + 1) * size)
        r = j * heads + h
        grad = total[:, cols]
        unit = attended[rows, cols].astype(F32)
        both = (grad * unit).astype(BF16)
        yield True
        mean = mm(both, ones, NN)
        yield True
        grad = ((grad - unit * mean) * scales[:, r : r + 1]).astype(BF16)
        yield True
        term = mm(grown_rows[cols, rows], grad, NN)
        yield True
        mixed_grad[rows, cols] = grad
        at = slice((h * chunks + j) * width, (h * chunks + j + 1) * width)
        later = states[h]
        exits[at, :] = jnp.zeros((width, width), BF16) if later is None else later.astype(BF16)
        end = jnp.exp(run[r : r + 1, size - 1 : size])
        states[h] = term if later is None else term + later * end
        yield True

    for j in reversed(range(chunks)):
        rows = slice(j * size, (j + 1) * size)
        total = partial[rows, :]
        for i, piece in enumerate(pieces):
            total = total + mm(
                piece[rows, :], rows_of_weight[i * part : (i + 1) * part, :], NN
            )
        together(step(j, h, total) for h in range(heads))
    for h in range(heads):
        at = slice(h * width, (h + 1) * width)
        update[at, :] = states[h]
        packed[at, :] = states[h].astype(BF16)
    put_foot(packed, heads * width, block_totals(run, heads, width))


def back_body(
    heads, queries, keys, values, mixed_grad, tables, incoming, states, exits,
    query_grad, key_grad, value_grad,
):
    width = incoming.shape[1]
    size = tables.shape[2]
    chunks = tables.shape[1] // heads
    causal = lax.broadcasted_iota(jnp.int32, (size, size), 0) <= lax.broadcasted_iota(
        jnp.int32, (size, size), 1
    )
    below = causal_mask(size)
    run = tables[RUN]
    sums, grow, tails = run.T, tables[GROW].T, tables[TAIL].T

    def step(h, j, start):
        cols, rows = slice(h * width, (h + 1) * width), slice(j * size, (j + 1) * size)
        r = j * heads + h
        at = slice((h * chunks + j) * width, (h * chunks + j + 1) * width)
        grad, query = mixed_grad[rows, cols], queries[rows, cols]
        key, value = keys[rows, cols], values[rows, cols]
        weight, masked, turned = mm(key, query, NT), mm(value, grad, NT), mm(grad, value, NT)
        yield True
        decay = jnp.exp(
            jnp.where(causal, run[r : r + 1, :] - sums[:, r : r + 1], -jnp.inf)
        )
        weight, masked = (weight * decay).astype(BF16), (masked * decay).astype(BF16)
        yield True
        decay = jnp.exp(jnp.where(below, sums[:, r : r + 1] - run[r : r + 1, :], -jnp.inf))
        turned = (turned * decay).astype(BF16)
        grown = (grad * grow[:, r : r + 1]).astype(BF16)
        state = ((states[at, :].astype(F32) + start) if j else start).astype(BF16)
        if j < chunks - 1:
            tail = tails[:, r : r + 1]
            value_tail, key_tail = (value * tail).astype(BF16), (key * tail).astype(BF16)
        yield True
        query_part = mm(turned, key, NN) + mm(grown, state, NT)
        key_part = mm(masked, query, NN)
        value_part = mm(weight, grad, NN)
        if j < chunks - 1:
            key_part = key_part + mm(value_tail, exits[at, :], NT)
            value_part = value_part + mm(key_tail, exits[at, :], NN)
        yield True
        query_grad[rows, cols] = query_part.astype(BF16)
        key_grad[rows, cols] = key_part.astype(BF16)
        value_grad[rows, cols] = value_part.astype(BF16)
        yield True

    for h in range(heads):
        starts = [incoming[h * width : (h + 1) * width, :]]
        for j in range(1, chunks):
            r = (j - 1) * heads + h
            starts.append(starts[-1] * grow[size - 1 : size, r : r + 1])
        together(step(h, j, starts[j]) for j in range(chunks))
        query_grad.send(h)
        key_grad.send(h)
        value_grad.send(h)


def final_body(
    heads, place, keys, values, tables, mine, theirs, other, key_part, value_part,
    key_grad, value_grad, outgoing,
):
    width = mine.shape[1]
    size = tables.shape[2]
    chunks = tables.shape[1] // heads
    enter(False, heads, place, mine, theirs, other, outgoing)
    tails = tables[TAIL_BLOCK].T
    def step(h, j, state):
        cols, rows = slice(h * width, (h + 1) * width), slice(j * size, (j + 1) * size)
        r = j * heads + h
        tail = tails[:, r : r + 1]
        value_tail = (values[rows, cols] * tail).astype(BF16)
        key_tail = (keys[rows, cols] * tail).astype(BF16)
        yield True
        key_sum, value_sum = mm(value_tail, state, NT), mm(key_tail, state, NN)
        yield True
        key_grad[rows, cols] = (key_part[rows, cols] + key_sum).astype(BF16)
        value_grad[rows, cols] = (value_part[rows, cols] + value_sum).astype(BF16)
        yield True

    for h in range(heads):
        state = outgoing[h * width : (h + 1) * width, :].astype(BF16)
        together(step(h, j, state) for j in range(chunks))
        key_grad.send(h)
        value_grad.send(h)


def fold_body(place, mine, low, middle, high, kept, sent):
    odd = place[2] % 2 == 1
    parts = [
        (mine[i].astype(F32) + part[...].astype(F32)).astype(BF16)
        for i, part in enumerate((low, middle, high))
    ]
    kept[0] = jnp.where(odd, parts[1], parts[0])
    kept[1] = parts[2]
    sent[0] = jnp.where(odd, parts[0], parts[1])
    sent[1] = parts[2]


def fold_again_body(place, kept, arrived, total, sent):
    turn = place[2]
    first = kept[0].astype(F32) + arrived[0].astype(F32)
    second = kept[1].astype(F32) + arrived[1].astype(F32)
    total[...] = jnp.where(turn == 2, second, first)
    sent[...] = jnp.where(turn == 0, second, first).astype(BF16)


def add_body(mine, arrived, out):
    out[...] = (mine[...].astype(F32) + arrived[...].astype(F32)).astype(BF16)


def cut_body(part, x, y, low, high, token, *rest):
    buffers, semaphores = rest[:2], rest[2]
    loads = [
        pltpu.make_async_copy(source, buffer, semaphores.at[i])
        for i, (source, buffer) in enumerate(
            ((x.at[:, :part], buffers[0]), (y.at[:, part:], buffers[1]))
        )
    ]
    stores = [
        pltpu.make_async_copy(buffer, target, semaphores.at[2 + i])
        for i, (buffer, target) in enumerate(((buffers[0], low), (buffers[1], high)))
    ]
    for load in loads:
        load.start()
    for load, store in zip(loads, stores):
        load.wait()
        store.start()
    token[...] = jnp.zeros(token.shape, F32)
    for store in stores:
        store.wait()


def hop(value, step, turns, chips, count):
    moves = [
        (s * count + y, ((s // 2 ^ step) * 2 + s % 2) * count + y)
        for s in range(2 * chips)
        for y in range(count)
        if s // 2 ^ y in turns
    ]
    return lax.ppermute(value, ("seq", "head"), moves)


class Chain:
    def __init__(self, line, forward, heads, chips, update, packed):
        self.line, self.forward, self.heads, self.chips = line, forward, heads, chips
        self.update, self.packed = update, packed
        self.other = self.swap(packed)

    def swap(self, value):
        return lax.ppermute(value, "seq", [(i, i ^ 1) for i in range(2 * self.chips)])

    def send(self):
        rows, width = self.update.shape
        self.half = (rows // 2, width)
        message, = self.line.call(
            functools.partial(combine_body, self.forward, self.heads),
            [((rows // 2 + foot_rows(self.heads), width), BF16)],
            self.update, self.packed, self.other,
            scratch=[pltpu.VMEM((rows, width), F32)], place=True,
        )
        self.line.held[self] = self.other
        self.arrived = [
            lax.ppermute(
                message, "seq",
                [(i, (i // 2 + k) % self.chips * 2 + i % 2) for i in range(2 * self.chips)],
            )
            for k in range(1, self.chips)
        ]

    def join(self):
        self.mine, = self.line.call(
            functools.partial(join_body, self.forward, self.heads, self.chips),
            [(self.half, BF16)], *self.arrived, place=True,
        )
        self.theirs = self.swap(self.mine)

    def done(self):
        self.line.held.pop(self)
        return self.mine, self.theirs, self.other


def on_device(seq_size, head_size, queries, keys, values, log_decay, out_weight, out_grad):
    length, columns = queries.shape
    heads = log_decay.shape[0]
    width = columns // heads
    size = 256 if length % 256 == 0 else length
    chunks = length // size
    chips = seq_size // 2
    near = head_size == 4 and chips == 4
    seq, head = lax.axis_index("seq"), lax.axis_index("head")
    turn = (seq // 2) ^ head
    block = out_grad.shape[1]
    part = block // 2
    move = lambda a, k: lax.ppermute(a, "head", [(i, i ^ k) for i in range(head_size)])
    if near:
        x, y = move(out_grad, 1), move(out_grad, 2)
    else:
        whole = lax.all_gather(out_grad, "head", axis=1, tiled=True)
    state = ((heads * width, width), F32)
    message = ((heads * width + foot_rows(heads), width), BF16)
    rows = (length, columns)
    line = Line()
    held = line.held

    chunk_states = ((heads * chunks * width, width), BF16)
    tables, update, packed, states = line.call(
        state_body, [((5, chunks * heads, size), F32), state, message, chunk_states],
        keys, values, log_decay, fetch={2: 1, 0: heads, 1: heads}, store={3: (heads, 0)},
    )
    forward = Chain(line, True, heads, chips, update, packed)
    pass
    forward.send()
    mixed, grown_rows = line.call(
        local_body, [(rows, F32), ((columns, length), BF16)], queries, keys, values, tables, states,
        fetch={0: heads, 1: heads, 2: heads, 4: (heads, 0)}, store={1: (heads, 0)},
    )
    held.update(mixed=mixed)
    forward.join()
    entering = forward.done()
    held.pop("mixed")
    attended, inverse, incoming = line.call(
        functools.partial(norm_body, heads),
        [(rows, BF16), ((chunks * heads, size), F32), state],
        mixed, queries, tables, *entering, place=True,
        fetch={1: (chunks, 0)}, store={0: (chunks, 0)},
    )
    held.update(inverse=inverse, incoming=incoming)
    swap = lambda a: lax.ppermute(a, "seq", [(i, i ^ 1) for i in range(2 * chips)])
    shape = (part, columns)
    if near:
        low, high, _ = line.call(
            functools.partial(cut_body, part),
            [((length, part), BF16)] * 2 + [((8, 128), F32)], x, y,
            scratch=[pltpu.VMEM((length, part), BF16)] * 2 + [pltpu.SemaphoreType.DMA((4,))],
            raw=(0, 1), raw_out=(0, 1), loose=(0, 1),
        )
        diagonal = [move(low, 2), move(high, 1)]
        products, *theirs, partial = line.call(
            functools.partial(early_body, size),
            [((3,) + shape, BF16)] + [(shape, BF16)] * 3 + [(rows, F32)],
            out_weight, attended, out_grad, x, y,
            scratch=[pltpu.VMEM((3 * block, columns), BF16), pltpu.SemaphoreType.DMA((3,))],
            place=True, raw=(0,), fetch={1: 1, 2: 1, 3: 1, 4: 1}, loose=(3, 4),
            store={0: (1, 0)},
        )
        arrived = [swap(a) for a in theirs]
        held["partial"] = partial
        kept, sent = line.call(
            fold_body, [((2,) + shape, BF16), ((2,) + shape, BF16)],
            products, *arrived, place=True, fetch={0: (1, 0), 1: (1, 0), 2: (1, 0), 3: (1, 0)},
            loose=(1, 2, 3), store={0: (1, 0), 1: (1, 0)},
        )
        arrived = hop(sent, 1, (0, 1, 2, 3), chips, head_size)
        held.pop("partial")
        mixed_grad, back_update, back_packed, exits, last, theirs = line.call(
            functools.partial(late_body, heads, 2),
            [(rows, BF16), state, message, chunk_states, (shape, BF16), (shape, BF16)],
            out_weight, attended, *diagonal, partial, inverse, grown_rows, tables,
            scratch=[pltpu.VMEM((block, columns), BF16), pltpu.SemaphoreType.DMA((1,))],
            place=True, raw=(0,), fetch={1: 1, 2: 1, 3: 1, 6: (1, 0)}, loose=(2, 3),
            store={3: (heads, 0)},
        )
        held["last"] = last
        last_arrived = swap(theirs)
    else:
        partial, = line.call(
            functools.partial(head_grad_body, size), [(rows, F32)],
            out_weight, whole,
        )
        mixed_grad, back_update, back_packed, exits = line.call(
            functools.partial(late_body, heads, 0), [(rows, BF16), state, message, chunk_states],
            out_weight, attended, partial, inverse, grown_rows, tables, place=True,
        )
    back = Chain(line, False, heads, chips, back_update, back_packed)
    held.pop("inverse")
    held["mixed_grad"] = mixed_grad
    held["update"] = back_update
    back.send()
    held.pop("update")
    if near:
        held.pop("last")
        last, = line.call(add_body, [(shape, BF16)], last, last_arrived)
        held["last"] = last
        last_arrived = hop(last, 1, (0, 2), chips, head_size)
        total, sent = line.call(
            fold_again_body, [(shape, F32), (shape, BF16)], kept, arrived, place=True,
            fetch={0: (1, 0), 1: (1, 0)}, loose=(1,),
        )
        arrived = hop(sent, 2, (0, 2, 3), chips, head_size)
    query_grad, key_part, value_part = line.call(
        functools.partial(back_body, heads), [(rows, BF16), (rows, BF16), (rows, BF16)],
        queries, keys, values, mixed_grad, tables, incoming, states, exits,
        fetch={0: heads, 1: heads, 2: heads, 6: (heads, 0), 7: (heads, 0)},
        store={i: heads for i in range(3)},
    )
    for name in ("mixed_grad", "incoming"):
        held.pop(name)
    back.join()
    if near:
        held.pop("last")
        last, = line.call(add_body, [(shape, BF16)], last, last_arrived)
        last_arrived = hop(last, 2, (1,), chips, head_size)
    key_grad, value_grad = line.call(
        functools.partial(final_body, heads), [(rows, BF16)] * 2,
        keys, values, tables, *back.done(), key_part, value_part,
        scratch=[pltpu.VMEM((heads * width, width), F32)], place=True,
        fetch={0: heads, 1: heads, 6: heads, 7: heads}, store={0: heads, 1: heads},
    )
    if near:
        weight_grad = jnp.where(
            turn == 3, last.astype(F32) + last_arrived.astype(F32),
            total + arrived.astype(F32),
        )
    else:
        weight_grad = lax.psum_scatter(
            mm(whole, attended, TN), "seq", scatter_dimension=0, tiled=True
        )
    return attended, query_grad, key_grad, value_grad, weight_grad.astype(BF16)


def solution(mesh):
    block = P("seq", "head")
    return jax.shard_map(
        functools.partial(on_device, mesh.shape["seq"], mesh.shape["head"]),
        mesh=mesh,
        in_specs=(block, block, block, P("head", "seq"), P(None, "head"), block),
        out_specs=(block,) * 5,
        check_vma=False,
    )
```

```python
import functools

import jax
import jax.numpy as jnp
from jax import lax
from jax.experimental import pallas as pl
from jax.experimental.pallas import tpu as pltpu
from jax.sharding import PartitionSpec as P

HIGH = lax.Precision.HIGHEST
F32 = jnp.float32
BF16 = jnp.bfloat16
VMEM = pl.BlockSpec(memory_space=pltpu.VMEM)
ANY = pl.BlockSpec(memory_space=pl.ANY)
NN = (((1,), (0,)), ((), ()))
NT = (((1,), (1,)), ((), ()))
TN = (((0,), (0,)), ((), ()))


def mm(left, right, dims):
    return lax.dot_general(left, right, dims, preferred_element_type=F32)


class Fetch:
    def __init__(self, source, buffer, semaphores, axis=1):
        self.buffer, self.axis = buffer, axis
        self.count = semaphores.shape[0]
        self.step = buffer.shape[axis] // self.count
        at = [
            (slice(None),) * axis + (slice(i * self.step, (i + 1) * self.step),)
            for i in range(self.count)
        ]
        self.copies = [
            pltpu.make_async_copy(source.at[p], buffer.at[p], semaphores.at[i])
            for i, p in enumerate(at)
        ]
        self.waiting = set(range(self.count))

        self.shape = buffer.shape

    def __getitem__(self, index):
        span = index[self.axis] if isinstance(index, tuple) else slice(None)
        first, last = span.start or 0, span.stop or self.buffer.shape[self.axis]
        wanted = {i for i in self.waiting if first < (i + 1) * self.step and i * self.step < last}
        if wanted and 0 not in self.waiting or len(wanted) > 1:
            wanted = set(self.waiting)
        for i in sorted(wanted):
            self.copies[i].wait()
        self.waiting -= wanted
        return self.buffer[index]


def start_all(*fetches):
    for i in range(max(f.count for f in fetches)):
        for f in fetches:
            if i < f.count:
                f.copies[i].start()


class Store(Fetch):
    def __init__(self, target, buffer, semaphores, axis=1):
        self.buffer, self.axis = buffer, axis
        self.count = semaphores.shape[0]
        self.step = buffer.shape[axis] // self.count
        at = [
            (slice(None),) * axis + (slice(i * self.step, (i + 1) * self.step),)
            for i in range(self.count)
        ]
        self.copies = [
            pltpu.make_async_copy(buffer.at[p], target.at[p], semaphores.at[i])
            for i, p in enumerate(at)
        ]

        self.shape, self.ready, self.left = buffer.shape, [], set(range(self.count))

    def __setitem__(self, index, value):
        self.buffer[index] = value

    def send(self, i):
        self.ready.append(i)
        if len(self.ready) * 2 >= self.count:
            self.start(self.ready)
            self.ready = []

    def start(self, blocks):
        for i in blocks:
            self.copies[i].start()
            self.left.remove(i)

    def finish(self):
        self.start(sorted(self.left))
        for copy in self.copies:
            copy.wait()


GROUP = 4


def together(steps):
    steps = list(steps)
    for i in range(0, len(steps), GROUP):
        running = steps[i : i + GROUP]
        while running:
            running = [step for step in running if next(step, None) is not None]


def here():
    seq, head = lax.axis_index("seq"), lax.axis_index("head")
    return seq >> 1, seq & 1, (seq >> 1) ^ head, head


class Line:
    def __init__(self):
        self.last = None
        self.held = {}

    def call(self, body, outs, *args, scratch=(), place=False, fetch={}, store={}, raw=(), raw_out=(), loose=()):
        fetch = {i: f if isinstance(f, tuple) else (f, 1) for i, f in fetch.items()}
        store = {i: f if isinstance(f, tuple) else (f, 1) for i, f in store.items()}
        shapes = [
            (pltpu.HBM if i in store or i in raw_out else jax.ShapeDtypeStruct)(shape, dtype)
            for i, (shape, dtype) in enumerate(outs)
        ]
        seen = {id(a) for a in args}
        extra = [] if self.last is None else [self.last]
        extra += [a for a in self.held.values()]
        extra = [a for a in extra if id(a) not in seen]
        count, more, results = len(args), len(extra), len(outs)
        hbm = pl.BlockSpec(memory_space=pltpu.HBM)
        specs = [ANY if i in loose else hbm if i in fetch else hbm if i in raw else VMEM for i in range(count)]
        buffers = []
        for i, (blocks, _) in fetch.items():
            buffers += [pltpu.VMEM(args[i].shape, args[i].dtype), pltpu.SemaphoreType.DMA((blocks,))]
        for i, (blocks, _) in store.items():
            buffers += [pltpu.VMEM(*outs[i]), pltpu.SemaphoreType.DMA((blocks,))]

        def kernel(*refs):
            ins, out = list(refs[:count]), list(refs[count + more : count + more + results])
            rest = list(refs[count + more + results :])
            for i, (_, axis) in fetch.items():
                ins[i] = Fetch(ins[i], rest.pop(0), rest.pop(0), axis)
            for i, (_, axis) in store.items():
                out[i] = Store(out[i], rest.pop(0), rest.pop(0), axis)
            if fetch:
                start_all(*[ins[i] for i in fetch])
            if place:
                ins = [here()] + ins
            body(*ins, *out, *rest)
            for i in store:
                out[i].finish()

        args = [
            pltpu.with_memory_space_constraint(a, pltpu.HBM) if (i in fetch or i in raw) and i not in loose else a
            for i, a in enumerate(args)
        ]
        values = pl.pallas_call(
            kernel,
            out_shape=shapes,
            in_specs=specs + [ANY] * more,
            out_specs=[hbm if i in store or i in raw_out else VMEM for i in range(results)],
            scratch_shapes=buffers + list(scratch),
            compiler_params=pltpu.CompilerParams(vmem_limit_bytes=24 * 1024 * 1024),
        )(*args, *extra)
        least = min(range(results), key=lambda i: values[i].size * values[i].dtype.itemsize)
        self.last = values[least]
        if least in store or least in raw_out:
            self.last = pltpu.with_memory_space_constraint(self.last, pltpu.HBM)
        return values


def foot_rows(heads):
    return -(-3 * heads // 16) * 16


def put_foot(out, base, totals):
    rows = []
    for total in totals:
        for _ in range(3):
            part = total.astype(BF16)
            rows.append(part.astype(F32))
            total = total - part.astype(F32)
    width = rows[0].shape[1]
    fill = foot_rows(len(totals)) - len(rows)
    if fill:
        rows.append(jnp.zeros((fill, width), F32))
    out[base:, :] = jnp.concatenate(rows, axis=0).astype(BF16)


def get_foot(message, base, heads):
    foot = message[base:, :].astype(F32)
    return [
        foot[3 * h : 3 * h + 1, :] + foot[3 * h + 1 : 3 * h + 2, :] + foot[3 * h + 2 : 3 * h + 3, :]
        for h in range(heads)
    ]


RUN, GROW, TAIL, GROW_BLOCK, TAIL_BLOCK = range(5)


def state_body(keys, values, log_decay, tables, update, packed, states):
    heads, size = log_decay.buffer.shape[0], tables.shape[2]
    chunks = tables.shape[1] // heads
    width = update.shape[1]
    upper = (
        lax.broadcasted_iota(jnp.int32, (size, size), 0)
        <= lax.broadcasted_iota(jnp.int32, (size, size), 1)
    ).astype(F32)
    pieces = jnp.concatenate(
        [log_decay[:, j * size : (j + 1) * size] for j in range(chunks)], axis=0
    )
    run = lax.dot_general(pieces, upper, NN, precision=HIGH, preferred_element_type=F32)
    ends = [run[j * heads : (j + 1) * heads, size - 1 : size] for j in range(chunks)]
    before, after = [jnp.zeros((heads, 1), F32)], [jnp.zeros((heads, 1), F32)]
    for j in range(chunks - 1):
        before.append(before[-1] + ends[j])
        after.append(after[-1] + ends[chunks - 1 - j])
    before = jnp.concatenate(before, axis=0)
    after = jnp.concatenate(after[::-1], axis=0)
    left = run[:, size - 1 : size] - run
    tables[RUN] = run
    tables[GROW] = jnp.exp(run)
    tables[TAIL] = jnp.exp(left)
    tables[GROW_BLOCK] = jnp.exp(run + before)
    tables[TAIL_BLOCK] = jnp.exp(left + after)
    tail_columns = jnp.exp(left).T
    def product(h, j, terms):
        cols, rows = slice(h * width, (h + 1) * width), slice(j * size, (j + 1) * size)
        r = j * heads + h
        tail = (keys[rows, cols] * tail_columns[:, r : r + 1]).astype(BF16)
        value = values[rows, cols]
        yield True
        terms.append(mm(tail, value, TN))
        yield True

    for h in range(heads):
        cols = slice(h * width, (h + 1) * width)
        terms = []
        together(product(h, j, terms) for j in range(chunks))
        state = None
        for j in range(chunks):
            r = j * heads + h
            at = slice((h * chunks + j) * width, (h * chunks + j + 1) * width)
            states[at, :] = jnp.zeros((width, width), BF16) if j == 0 else state.astype(BF16)
            end = jnp.exp(run[r : r + 1, size - 1 : size])
            state = terms[j] if state is None else state * end + terms[j]
        states.send(h)
        update[cols, :] = state
        packed[cols, :] = state.astype(BF16)
    put_foot(packed, heads * width, block_totals(run, heads, width))


def block_totals(run, heads, width):
    chunks, size = run.shape[0] // heads, run.shape[1]
    ends = run[:, size - 1 : size]
    return [
        sum(
            jnp.broadcast_to(ends[j * heads + h : j * heads + h + 1, :], (1, width))
            for j in range(chunks)
        )
        for h in range(heads)
    ]


def combine_body(forward, heads, place, own, packed, other, out, whole):
    core = place[1]
    width = own.shape[1]
    rows = heads * width
    mine, theirs = get_foot(packed, rows, heads), get_foot(other, rows, heads)
    late = core == (1 if forward else 0)
    for h in range(heads):
        at = slice(h * width, (h + 1) * width)
        a, b = own[at, :], other[at, :].astype(F32)
        joined = jnp.where(late, a + jnp.exp(mine[h]) * b, b + jnp.exp(theirs[h]) * a)
        whole[at, :] = joined
    half = rows // 2
    out[:half, :] = whole[pl.ds(pl.multiple_of(core * half, half), half), :].astype(BF16)
    put_foot(out, half, [a + b for a, b in zip(mine, theirs)])


def join_body(forward, heads, chips, place, *refs):
    messages, out = refs[: chips - 1], refs[chips - 1]
    chip, core = place[0], place[1]
    half, width = out.shape
    feet = [get_foot(m, half, heads) for m in messages]
    spans = [jnp.zeros((1, width), F32)] * heads
    head_rows = half * 2 // heads
    groups = max(1, half // head_rows)
    total = [None] * groups
    for k in range(1, chips) if forward else range(chips - 1, 0, -1):
        used = (k <= chip) if forward else (k > chip)
        for g in range(groups):
            span = spans[0] if heads == 1 else jnp.where(core == 0, spans[g], spans[groups + g])
            factor = jnp.where(used, jnp.exp(span), 0.0)
            at = slice(g * half // groups, (g + 1) * half // groups)
            term = factor * messages[k - 1][at, :].astype(F32)
            total[g] = term if total[g] is None else total[g] + term
        spans = [span + foot for span, foot in zip(spans, feet[k - 1])]
    for g in range(groups):
        out[g * half // groups : (g + 1) * half // groups, :] = total[g].astype(BF16)


def enter(forward, heads, place, mine, theirs, other, out):
    core = place[1]
    half, width = mine.shape
    rows = 2 * half
    out[pl.ds(pl.multiple_of(core * half, half), half), :] = mine[...].astype(F32)
    out[pl.ds(pl.multiple_of((1 - core) * half, half), half), :] = theirs[...].astype(F32)
    totals = get_foot(other, rows, heads)
    late = core == (1 if forward else 0)
    for h in range(heads):
        at = slice(h * width, (h + 1) * width)
        now = out[at, :]
        moved = other[at, :].astype(F32) + jnp.exp(totals[h]) * now
        out[at, :] = jnp.where(late, moved, now)


def causal_mask(size):
    return lax.broadcasted_iota(jnp.int32, (size, size), 0) >= lax.broadcasted_iota(
        jnp.int32, (size, size), 1
    )


def decay_of(run, columns, r, causal):
    return jnp.exp(jnp.where(causal, columns[:, r : r + 1] - run[r : r + 1, :], -jnp.inf))


def local_body(queries, keys, values, tables, states, mixed, grown_rows):
    size = tables.shape[2]
    length, columns = mixed.shape
    chunks = length // size
    heads = tables.shape[1] // chunks
    width = columns // heads
    causal = causal_mask(size)
    run = tables[RUN]
    sums, grow = run.T, tables[GROW].T
    def step(h, j):
        cols, rows = slice(h * width, (h + 1) * width), slice(j * size, (j + 1) * size)
        r = j * heads + h
        query, key, value = queries[rows, cols], keys[rows, cols], values[rows, cols]
        scores = mm(query, key, NT)
        grown = (query * grow[:, r : r + 1]).astype(BF16)
        yield True
        weight = (scores * decay_of(run, sums, r, causal)).astype(BF16)
        turned = grown.T
        yield True
        out = mm(weight, value, NN)
        if j:
            at = slice((h * chunks + j) * width, (h * chunks + j + 1) * width)
            out = out + mm(grown, states[at, :], NN)
        yield True
        grown_rows[cols, rows] = turned
        mixed[rows, cols] = out
        yield True

    for h in range(heads):
        together(step(h, j) for j in range(chunks))
        grown_rows.send(h)


def norm_body(
    heads, place, mixed, queries, tables, mine, theirs, other, attended, inverse, incoming
):
    width = mine.shape[1]
    size = tables.shape[2]
    chunks = tables.shape[1] // heads
    enter(True, heads, place, mine, theirs, other, incoming)
    grow = tables[GROW_BLOCK].T
    ones = jnp.full((width, width), 1.0 / width, BF16)
    lane = lax.broadcasted_iota(jnp.int32, (size, width), 1)
    low = [incoming[h * width : (h + 1) * width, :].astype(BF16) for h in range(heads)]
    def step(j, h, scales):
        cols, rows = slice(h * width, (h + 1) * width), slice(j * size, (j + 1) * size)
        r = j * heads + h
        grown = (queries[rows, cols] * grow[:, r : r + 1]).astype(BF16)
        yield True
        total = mixed[rows, cols] + mm(grown, low[h], NN)
        square = (total * total).astype(BF16)
        yield True
        scale = lax.rsqrt(mm(square, ones, NN) + 1e-05)
        yield True
        scales[0] = jnp.where(lane == h, scale, scales[0])
        attended[rows, cols] = (total * scale).astype(BF16)
        yield True

    for j in range(chunks):
        scales = [jnp.zeros((size, width), F32)]
        together(step(j, h, scales) for h in range(heads))
        inverse[j * heads : (j + 1) * heads, :] = scales[0].T[:heads, :]
        attended.send(j)


def head_grad_body(size, weight, whole, out):
    for t in range(out.shape[0] // size):
        rows = slice(t * size, (t + 1) * size)
        out[rows, :] = mm(whole[rows, :], weight[...], NN)


def weight_copies(head, blocks, weight, rows_of_weight, semaphores):
    depth = rows_of_weight.shape[0] // len(blocks)
    return [
        pltpu.make_async_copy(
            weight.at[pl.ds(pl.multiple_of((head ^ k) * depth, depth), depth), :],
            rows_of_weight.at[i * depth : (i + 1) * depth, :],
            semaphores.at[i],
        )
        for i, k in enumerate(blocks)
    ]


def early_body(size, place, weight, attended, *refs):
    pieces, mine, theirs, out, rows_of_weight, semaphores = (
        refs[:3], refs[3], refs[4:7], refs[7], refs[8], refs[9]
    )
    _, core, _, head = place
    part = mine.shape[1]
    copies = weight_copies(head, (0, 1, 2), weight, rows_of_weight, semaphores)
    for copy in copies:
        copy.start()
    for i, piece in enumerate(pieces):
        product = mm(piece[...], attended[...], TN)
        low, high = product[:part, :].astype(BF16), product[part:, :].astype(BF16)
        mine[i] = jnp.where(core == 0, low, high)
        theirs[i][...] = jnp.where(core == 0, high, low)
    for copy in copies:
        copy.wait()
    for t in range(out.shape[0] // size):
        rows = slice(t * size, (t + 1) * size)
        out[rows, :] = sum(
            mm(piece[rows, :], rows_of_weight[2 * part * i : 2 * part * (i + 1), :], NN)
            for i, piece in enumerate(pieces)
        )


def late_body(heads, number, place, weight, attended, *refs):
    pieces = refs[:number]
    refs = refs[number:]
    partial, inverse, grown_rows, tables, mixed_grad, update, packed, exits = refs[:8]
    width = update.shape[1]
    size = tables.shape[2]
    chunks = tables.shape[1] // heads
    if number:
        mine, theirs, rows_of_weight, semaphores = refs[8:]
        _, core, _, head = place
        part = mine.shape[0]
        copy, = weight_copies(head, (3,), weight, rows_of_weight, semaphores)
        copy.start()
        low, high = [mm(p[...], attended[...], TN).astype(BF16) for p in pieces]
        mine[...] = jnp.where(core == 0, low, high)
        theirs[...] = jnp.where(core == 0, high, low)
        copy.wait()
    ones = jnp.full((width, width), 1.0 / width, BF16)
    states = [None] * heads
    run = tables[RUN]
    scales = inverse[...].T

    def step(j, h, total):
        cols, rows = slice(h * width, (h + 1) * width), slice(j * size, (j + 1) * size)
        r = j * heads + h
        grad = total[:, cols]
        unit = attended[rows, cols].astype(F32)
        both = (grad * unit).astype(BF16)
        yield True
        mean = mm(both, ones, NN)
        yield True
        grad = ((grad - unit * mean) * scales[:, r : r + 1]).astype(BF16)
        yield True
        term = mm(grown_rows[cols, rows], grad, NN)
        yield True
        mixed_grad[rows, cols] = grad
        at = slice((h * chunks + j) * width, (h * chunks + j + 1) * width)
        later = states[h]
        exits[at, :] = jnp.zeros((width, width), BF16) if later is None else later.astype(BF16)
        end = jnp.exp(run[r : r + 1, size - 1 : size])
        states[h] = term if later is None else term + later * end
        yield True

    for j in reversed(range(chunks)):
        rows = slice(j * size, (j + 1) * size)
        total = partial[rows, :]
        for i, piece in enumerate(pieces):
            total = total + mm(
                piece[rows, :], rows_of_weight[i * part : (i + 1) * part, :], NN
            )
        together(step(j, h, total) for h in range(heads))
    for h in range(heads):
        at = slice(h * width, (h + 1) * width)
        update[at, :] = states[h]
        packed[at, :] = states[h].astype(BF16)
    put_foot(packed, heads * width, block_totals(run, heads, width))


def back_body(
    heads, queries, keys, values, mixed_grad, tables, incoming, states, exits,
    query_grad, key_grad, value_grad,
):
    width = incoming.shape[1]
    size = tables.shape[2]
    chunks = tables.shape[1] // heads
    causal = lax.broadcasted_iota(jnp.int32, (size, size), 0) <= lax.broadcasted_iota(
        jnp.int32, (size, size), 1
    )
    below = causal_mask(size)
    run = tables[RUN]
    sums, grow, tails = run.T, tables[GROW].T, tables[TAIL].T

    def step(h, j, start):
        cols, rows = slice(h * width, (h + 1) * width), slice(j * size, (j + 1) * size)
        r = j * heads + h
        at = slice((h * chunks + j) * width, (h * chunks + j + 1) * width)
        grad, query = mixed_grad[rows, cols], queries[rows, cols]
        key, value = keys[rows, cols], values[rows, cols]
        weight, masked, turned = mm(key, query, NT), mm(value, grad, NT), mm(grad, value, NT)
        yield True
        decay = jnp.exp(
            jnp.where(causal, run[r : r + 1, :] - sums[:, r : r + 1], -jnp.inf)
        )
        weight, masked = (weight * decay).astype(BF16), (masked * decay).astype(BF16)
        yield True
        decay = jnp.exp(jnp.where(below, sums[:, r : r + 1] - run[r : r + 1, :], -jnp.inf))
        turned = (turned * decay).astype(BF16)
        grown = (grad * grow[:, r : r + 1]).astype(BF16)
        state = ((states[at, :].astype(F32) + start) if j else start).astype(BF16)
        if j < chunks - 1:
            tail = tails[:, r : r + 1]
            value_tail, key_tail = (value * tail).astype(BF16), (key * tail).astype(BF16)
        yield True
        query_part = mm(turned, key, NN) + mm(grown, state, NT)
        key_part = mm(masked, query, NN)
        value_part = mm(weight, grad, NN)
        if j < chunks - 1:
            key_part = key_part + mm(value_tail, exits[at, :], NT)
            value_part = value_part + mm(key_tail, exits[at, :], NN)
        yield True
        query_grad[rows, cols] = query_part.astype(BF16)
        key_grad[rows, cols] = key_part.astype(BF16)
        value_grad[rows, cols] = value_part.astype(BF16)
        yield True

    for h in range(heads):
        starts = [incoming[h * width : (h + 1) * width, :]]
        for j in range(1, chunks):
            r = (j - 1) * heads + h
            starts.append(starts[-1] * grow[size - 1 : size, r : r + 1])
        together(step(h, j, starts[j]) for j in range(chunks))
        query_grad.send(h)
        key_grad.send(h)
        value_grad.send(h)


def final_body(
    heads, place, keys, values, tables, mine, theirs, other, key_part, value_part,
    key_grad, value_grad, outgoing,
):
    width = mine.shape[1]
    size = tables.shape[2]
    chunks = tables.shape[1] // heads
    enter(False, heads, place, mine, theirs, other, outgoing)
    tails = tables[TAIL_BLOCK].T
    def step(h, j, state):
        cols, rows = slice(h * width, (h + 1) * width), slice(j * size, (j + 1) * size)
        r = j * heads + h
        tail = tails[:, r : r + 1]
        value_tail = (values[rows, cols] * tail).astype(BF16)
        key_tail = (keys[rows, cols] * tail).astype(BF16)
        yield True
        key_sum, value_sum = mm(value_tail, state, NT), mm(key_tail, state, NN)
        yield True
        key_grad[rows, cols] = (key_part[rows, cols] + key_sum).astype(BF16)
        value_grad[rows, cols] = (value_part[rows, cols] + value_sum).astype(BF16)
        yield True

    for h in range(heads):
        state = outgoing[h * width : (h + 1) * width, :].astype(BF16)
        together(step(h, j, state) for j in range(chunks))
        key_grad.send(h)
        value_grad.send(h)


def fold_body(place, mine, low, middle, high, kept, sent):
    odd = place[2] % 2 == 1
    parts = [
        (mine[i].astype(F32) + part[...].astype(F32)).astype(BF16)
        for i, part in enumerate((low, middle, high))
    ]
    kept[0] = jnp.where(odd, parts[1], parts[0])
    kept[1] = parts[2]
    sent[0] = jnp.where(odd, parts[0], parts[1])
    sent[1] = parts[2]


def fold_again_body(place, kept, arrived, total, sent):
    turn = place[2]
    first = kept[0].astype(F32) + arrived[0].astype(F32)
    second = kept[1].astype(F32) + arrived[1].astype(F32)
    total[...] = jnp.where(turn == 2, second, first)
    sent[...] = jnp.where(turn == 0, second, first).astype(BF16)


def add_body(mine, arrived, out):
    out[...] = (mine[...].astype(F32) + arrived[...].astype(F32)).astype(BF16)


def cut_body(span, block, out, token):
    out[...] = block[:, span]
    token[...] = jnp.zeros(token.shape, F32)


def hop(value, step, turns, chips, count):
    moves = [
        (s * count + y, ((s // 2 ^ step) * 2 + s % 2) * count + y)
        for s in range(2 * chips)
        for y in range(count)
        if s // 2 ^ y in turns
    ]
    return lax.ppermute(value, ("seq", "head"), moves)


class Chain:
    def __init__(self, line, forward, heads, chips, update, packed):
        self.line, self.forward, self.heads, self.chips = line, forward, heads, chips
        self.update, self.packed = update, packed
        self.other = self.swap(packed)

    def swap(self, value):
        return lax.ppermute(value, "seq", [(i, i ^ 1) for i in range(2 * self.chips)])

    def send(self):
        rows, width = self.update.shape
        self.half = (rows // 2, width)
        message, = self.line.call(
            functools.partial(combine_body, self.forward, self.heads),
            [((rows // 2 + foot_rows(self.heads), width), BF16)],
            self.update, self.packed, self.other,
            scratch=[pltpu.VMEM((rows, width), F32)], place=True,
        )
        self.line.held[self] = self.other
        self.arrived = [
            lax.ppermute(
                message, "seq",
                [(i, (i // 2 + k) % self.chips * 2 + i % 2) for i in range(2 * self.chips)],
            )
            for k in range(1, self.chips)
        ]

    def join(self):
        self.mine, = self.line.call(
            functools.partial(join_body, self.forward, self.heads, self.chips),
            [(self.half, BF16)], *self.arrived, place=True,
        )
        self.theirs = self.swap(self.mine)

    def done(self):
        self.line.held.pop(self)
        return self.mine, self.theirs, self.other


def on_device(seq_size, head_size, queries, keys, values, log_decay, out_weight, out_grad):
    length, columns = queries.shape
    heads = log_decay.shape[0]
    width = columns // heads
    size = 256 if length % 256 == 0 else length
    chunks = length // size
    chips = seq_size // 2
    near = head_size == 4 and chips == 4
    seq, head = lax.axis_index("seq"), lax.axis_index("head")
    turn = (seq // 2) ^ head
    block = out_grad.shape[1]
    part = block // 2
    move = lambda a, k: lax.ppermute(a, "head", [(i, i ^ k) for i in range(head_size)])
    if near:
        x, y = move(out_grad, 1), move(out_grad, 2)
    else:
        whole = lax.all_gather(out_grad, "head", axis=1, tiled=True)
    state = ((heads * width, width), F32)
    message = ((heads * width + foot_rows(heads), width), BF16)
    rows = (length, columns)
    line = Line()
    held = line.held

    chunk_states = ((heads * chunks * width, width), BF16)
    tables, update, packed, states = line.call(
        state_body, [((5, chunks * heads, size), F32), state, message, chunk_states],
        keys, values, log_decay, fetch={2: 1, 0: heads, 1: heads}, store={3: (heads, 0)},
    )
    forward = Chain(line, True, heads, chips, update, packed)
    pass
    forward.send()
    mixed, grown_rows = line.call(
        local_body, [(rows, F32), ((columns, length), BF16)], queries, keys, values, tables, states,
        fetch={0: heads, 1: heads, 2: heads, 4: (heads, 0)}, store={1: (heads, 0)},
    )
    held.update(mixed=mixed)
    forward.join()
    entering = forward.done()
    held.pop("mixed")
    attended, inverse, incoming = line.call(
        functools.partial(norm_body, heads),
        [(rows, BF16), ((chunks * heads, size), F32), state],
        mixed, queries, tables, *entering, place=True,
        fetch={1: (chunks, 0)}, store={0: (chunks, 0)},
    )
    held.update(inverse=inverse, incoming=incoming)
    swap = lambda a: lax.ppermute(a, "seq", [(i, i ^ 1) for i in range(2 * chips)])
    shape = (part, columns)
    if near:
        cut = [((length, part), BF16), ((8, 128), F32)]
        low, _ = line.call(functools.partial(cut_body, slice(0, part)), cut, x)
        diagonal = [move(low, 2)]
        high, _ = line.call(functools.partial(cut_body, slice(part, block)), cut, y)
        diagonal.append(move(high, 1))
        products, *theirs, partial = line.call(
            functools.partial(early_body, size),
            [((3,) + shape, BF16)] + [(shape, BF16)] * 3 + [(rows, F32)],
            out_weight, attended, out_grad, x, y,
            scratch=[pltpu.VMEM((3 * block, columns), BF16), pltpu.SemaphoreType.DMA((3,))],
            place=True, raw=(0,), fetch={1: 1, 2: 1, 3: 1, 4: 1}, loose=(3, 4),
        )
        arrived = [swap(a) for a in theirs]
        held["partial"] = partial
        kept, sent = line.call(
            fold_body, [((2,) + shape, BF16), ((2,) + shape, BF16)],
            products, *arrived, place=True,
        )
        arrived = hop(sent, 1, (0, 1, 2, 3), chips, head_size)
        held.pop("partial")
        mixed_grad, back_update, back_packed, exits, last, theirs = line.call(
            functools.partial(late_body, heads, 2),
            [(rows, BF16), state, message, chunk_states, (shape, BF16), (shape, BF16)],
            out_weight, attended, *diagonal, partial, inverse, grown_rows, tables,
            scratch=[pltpu.VMEM((block, columns), BF16), pltpu.SemaphoreType.DMA((1,))],
            place=True, raw=(0,), fetch={1: 1, 2: 1, 3: 1, 6: (1, 0)}, loose=(2, 3),
            store={3: (heads, 0)},
        )
        held["last"] = last
        last_arrived = swap(theirs)
    else:
        partial, = line.call(
            functools.partial(head_grad_body, size), [(rows, F32)],
            out_weight, whole,
        )
        mixed_grad, back_update, back_packed, exits = line.call(
            functools.partial(late_body, heads, 0), [(rows, BF16), state, message, chunk_states],
            out_weight, attended, partial, inverse, grown_rows, tables, place=True,
        )
    back = Chain(line, False, heads, chips, back_update, back_packed)
    held.pop("inverse")
    held["mixed_grad"] = mixed_grad
    held["update"] = back_update
    back.send()
    held.pop("update")
    if near:
        held.pop("last")
        last, = line.call(add_body, [(shape, BF16)], last, last_arrived)
        held["last"] = last
        last_arrived = hop(last, 1, (0, 2), chips, head_size)
        total, sent = line.call(
            fold_again_body, [(shape, F32), (shape, BF16)], kept, arrived, place=True,
            fetch={0: (1, 0), 1: (1, 0)}, loose=(1,),
        )
        arrived = hop(sent, 2, (0, 2, 3), chips, head_size)
    query_grad, key_part, value_part = line.call(
        functools.partial(back_body, heads), [(rows, BF16), (rows, BF16), (rows, BF16)],
        queries, keys, values, mixed_grad, tables, incoming, states, exits,
        fetch={0: heads, 1: heads, 2: heads, 6: (heads, 0), 7: (heads, 0)},
        store={i: heads for i in range(3)},
    )
    for name in ("mixed_grad", "incoming"):
        held.pop(name)
    back.join()
    if near:
        held.pop("last")
        last, = line.call(add_body, [(shape, BF16)], last, last_arrived)
        last_arrived = hop(last, 2, (1,), chips, head_size)
    key_grad, value_grad = line.call(
        functools.partial(final_body, heads), [(rows, BF16)] * 2,
        keys, values, tables, *back.done(), key_part, value_part,
        scratch=[pltpu.VMEM((heads * width, width), F32)], place=True,
        fetch={0: heads, 1: heads, 6: heads, 7: heads}, store={0: heads, 1: heads},
    )
    if near:
        weight_grad = jnp.where(
            turn == 3, last.astype(F32) + last_arrived.astype(F32),
            total + arrived.astype(F32),
        )
    else:
        weight_grad = lax.psum_scatter(
            mm(whole, attended, TN), "seq", scatter_dimension=0, tiled=True
        )
    return attended, query_grad, key_grad, value_grad, weight_grad.astype(BF16)


def solution(mesh):
    block = P("seq", "head")
    return jax.shard_map(
        functools.partial(on_device, mesh.shape["seq"], mesh.shape["head"]),
        mesh=mesh,
        in_specs=(block, block, block, P("head", "seq"), P(None, "head"), block),
        out_specs=(block,) * 5,
        check_vma=False,
    )
```

```python
import functools

import jax
import jax.numpy as jnp
from jax import lax
from jax.experimental import pallas as pl
from jax.experimental.pallas import tpu as pltpu
from jax.sharding import PartitionSpec as P

HIGH = lax.Precision.HIGHEST
F32 = jnp.float32
BF16 = jnp.bfloat16
VMEM = pl.BlockSpec(memory_space=pltpu.VMEM)
ANY = pl.BlockSpec(memory_space=pl.ANY)
NN = (((1,), (0,)), ((), ()))
NT = (((1,), (1,)), ((), ()))
TN = (((0,), (0,)), ((), ()))


def mm(left, right, dims):
    return lax.dot_general(left, right, dims, preferred_element_type=F32)


class Fetch:
    def __init__(self, source, buffer, semaphores, axis=1):
        self.buffer, self.axis = buffer, axis
        self.count = semaphores.shape[0]
        self.step = buffer.shape[axis] // self.count
        at = [
            (slice(None),) * axis + (slice(i * self.step, (i + 1) * self.step),)
            for i in range(self.count)
        ]
        self.copies = [
            pltpu.make_async_copy(source.at[p], buffer.at[p], semaphores.at[i])
            for i, p in enumerate(at)
        ]
        self.waiting = set(range(self.count))

        self.shape = buffer.shape

    def __getitem__(self, index):
        span = index[self.axis] if isinstance(index, tuple) else slice(None)
        first, last = span.start or 0, span.stop or self.buffer.shape[self.axis]
        wanted = {i for i in self.waiting if first < (i + 1) * self.step and i * self.step < last}
        if wanted and 0 not in self.waiting or len(wanted) > 1:
            wanted = set(self.waiting)
        for i in sorted(wanted):
            self.copies[i].wait()
        self.waiting -= wanted
        return self.buffer[index]


def start_all(*fetches):
    for i in range(max(f.count for f in fetches)):
        for f in fetches:
            if i < f.count:
                f.copies[i].start()


class Store(Fetch):
    def __init__(self, target, buffer, semaphores, axis=1):
        self.buffer, self.axis = buffer, axis
        self.count = semaphores.shape[0]
        self.step = buffer.shape[axis] // self.count
        at = [
            (slice(None),) * axis + (slice(i * self.step, (i + 1) * self.step),)
            for i in range(self.count)
        ]
        self.copies = [
            pltpu.make_async_copy(buffer.at[p], target.at[p], semaphores.at[i])
            for i, p in enumerate(at)
        ]

        self.shape, self.ready, self.left = buffer.shape, [], set(range(self.count))

    def __setitem__(self, index, value):
        self.buffer[index] = value

    def send(self, i):
        self.ready.append(i)
        if len(self.ready) * 2 >= self.count:
            self.start(self.ready)
            self.ready = []

    def start(self, blocks):
        for i in blocks:
            self.copies[i].start()
            self.left.remove(i)

    def finish(self):
        self.start(sorted(self.left))
        for copy in self.copies:
            copy.wait()


GROUP = 4


def together(steps):
    steps = list(steps)
    for i in range(0, len(steps), GROUP):
        running = steps[i : i + GROUP]
        while running:
            running = [step for step in running if next(step, None) is not None]


def here():
    seq, head = lax.axis_index("seq"), lax.axis_index("head")
    return seq >> 1, seq & 1, (seq >> 1) ^ head, head


class Line:
    def __init__(self):
        self.last = None
        self.held = {}

    def call(self, body, outs, *args, scratch=(), place=False, fetch={}, store={}, raw=(), raw_out=(), loose=()):
        fetch = {i: f if isinstance(f, tuple) else (f, 1) for i, f in fetch.items()}
        store = {i: f if isinstance(f, tuple) else (f, 1) for i, f in store.items()}
        shapes = [
            (pltpu.HBM if i in store or i in raw_out else jax.ShapeDtypeStruct)(shape, dtype)
            for i, (shape, dtype) in enumerate(outs)
        ]
        seen = {id(a) for a in args}
        extra = [] if self.last is None else [self.last]
        extra += [a for a in self.held.values()]
        extra = [a for a in extra if id(a) not in seen]
        count, more, results = len(args), len(extra), len(outs)
        hbm = pl.BlockSpec(memory_space=pltpu.HBM)
        specs = [ANY if i in loose else hbm if i in fetch else hbm if i in raw else VMEM for i in range(count)]
        buffers = []
        for i, (blocks, _) in fetch.items():
            buffers += [pltpu.VMEM(args[i].shape, args[i].dtype), pltpu.SemaphoreType.DMA((blocks,))]
        for i, (blocks, _) in store.items():
            buffers += [pltpu.VMEM(*outs[i]), pltpu.SemaphoreType.DMA((blocks,))]

        def kernel(*refs):
            ins, out = list(refs[:count]), list(refs[count + more : count + more + results])
            rest = list(refs[count + more + results :])
            for i, (_, axis) in fetch.items():
                ins[i] = Fetch(ins[i], rest.pop(0), rest.pop(0), axis)
            for i, (_, axis) in store.items():
                out[i] = Store(out[i], rest.pop(0), rest.pop(0), axis)
            if fetch:
                start_all(*[ins[i] for i in fetch])
            if place:
                ins = [here()] + ins
            body(*ins, *out, *rest)
            for i in store:
                out[i].finish()

        args = [
            pltpu.with_memory_space_constraint(a, pltpu.HBM) if (i in fetch or i in raw) and i not in loose else a
            for i, a in enumerate(args)
        ]
        values = pl.pallas_call(
            kernel,
            out_shape=shapes,
            in_specs=specs + [ANY] * more,
            out_specs=[hbm if i in store or i in raw_out else VMEM for i in range(results)],
            scratch_shapes=buffers + list(scratch),
            compiler_params=pltpu.CompilerParams(vmem_limit_bytes=24 * 1024 * 1024),
        )(*args, *extra)
        least = min(range(results), key=lambda i: values[i].size * values[i].dtype.itemsize)
        self.last = values[least]
        if least in store or least in raw_out:
            self.last = pltpu.with_memory_space_constraint(self.last, pltpu.HBM)
        return values


def foot_rows(heads):
    return -(-3 * heads // 16) * 16


def put_foot(out, base, totals):
    rows = []
    for total in totals:
        for _ in range(3):
            part = total.astype(BF16)
            rows.append(part.astype(F32))
            total = total - part.astype(F32)
    width = rows[0].shape[1]
    fill = foot_rows(len(totals)) - len(rows)
    if fill:
        rows.append(jnp.zeros((fill, width), F32))
    out[base:, :] = jnp.concatenate(rows, axis=0).astype(BF16)


def get_foot(message, base, heads):
    foot = message[base:, :].astype(F32)
    return [
        foot[3 * h : 3 * h + 1, :] + foot[3 * h + 1 : 3 * h + 2, :] + foot[3 * h + 2 : 3 * h + 3, :]
        for h in range(heads)
    ]


RUN, GROW, TAIL, GROW_BLOCK, TAIL_BLOCK = range(5)


def state_body(keys, values, log_decay, tables, update, packed, states):
    heads, size = log_decay.buffer.shape[0], tables.shape[2]
    chunks = tables.shape[1] // heads
    width = update.shape[1]
    upper = (
        lax.broadcasted_iota(jnp.int32, (size, size), 0)
        <= lax.broadcasted_iota(jnp.int32, (size, size), 1)
    ).astype(F32)
    pieces = jnp.concatenate(
        [log_decay[:, j * size : (j + 1) * size] for j in range(chunks)], axis=0
    )
    run = lax.dot_general(pieces, upper, NN, precision=HIGH, preferred_element_type=F32)
    ends = [run[j * heads : (j + 1) * heads, size - 1 : size] for j in range(chunks)]
    before, after = [jnp.zeros((heads, 1), F32)], [jnp.zeros((heads, 1), F32)]
    for j in range(chunks - 1):
        before.append(before[-1] + ends[j])
        after.append(after[-1] + ends[chunks - 1 - j])
    before = jnp.concatenate(before, axis=0)
    after = jnp.concatenate(after[::-1], axis=0)
    left = run[:, size - 1 : size] - run
    tables[RUN] = run
    tables[GROW] = jnp.exp(run)
    tables[TAIL] = jnp.exp(left)
    tables[GROW_BLOCK] = jnp.exp(run + before)
    tables[TAIL_BLOCK] = jnp.exp(left + after)
    tail_columns = jnp.exp(left).T
    def product(h, j, terms):
        cols, rows = slice(h * width, (h + 1) * width), slice(j * size, (j + 1) * size)
        r = j * heads + h
        tail = (keys[rows, cols] * tail_columns[:, r : r + 1]).astype(BF16)
        value = values[rows, cols]
        yield True
        terms.append(mm(tail, value, TN))
        yield True

    for h in range(heads):
        cols = slice(h * width, (h + 1) * width)
        terms = []
        together(product(h, j, terms) for j in range(chunks))
        state = None
        for j in range(chunks):
            r = j * heads + h
            at = slice((h * chunks + j) * width, (h * chunks + j + 1) * width)
            states[at, :] = jnp.zeros((width, width), BF16) if j == 0 else state.astype(BF16)
            end = jnp.exp(run[r : r + 1, size - 1 : size])
            state = terms[j] if state is None else state * end + terms[j]
        states.send(h)
        update[cols, :] = state
        packed[cols, :] = state.astype(BF16)
    put_foot(packed, heads * width, block_totals(run, heads, width))


def block_totals(run, heads, width):
    chunks, size = run.shape[0] // heads, run.shape[1]
    ends = run[:, size - 1 : size]
    return [
        sum(
            jnp.broadcast_to(ends[j * heads + h : j * heads + h + 1, :], (1, width))
            for j in range(chunks)
        )
        for h in range(heads)
    ]


def combine_body(forward, heads, place, own, packed, other, out, whole):
    core = place[1]
    width = own.shape[1]
    rows = heads * width
    mine, theirs = get_foot(packed, rows, heads), get_foot(other, rows, heads)
    late = core == (1 if forward else 0)
    for h in range(heads):
        at = slice(h * width, (h + 1) * width)
        a, b = own[at, :], other[at, :].astype(F32)
        joined = jnp.where(late, a + jnp.exp(mine[h]) * b, b + jnp.exp(theirs[h]) * a)
        whole[at, :] = joined
    half = rows // 2
    out[:half, :] = whole[pl.ds(pl.multiple_of(core * half, half), half), :].astype(BF16)
    put_foot(out, half, [a + b for a, b in zip(mine, theirs)])


def join_body(forward, heads, chips, place, *refs):
    messages, out = refs[: chips - 1], refs[chips - 1]
    chip, core = place[0], place[1]
    half, width = out.shape
    feet = [get_foot(m, half, heads) for m in messages]
    spans = [jnp.zeros((1, width), F32)] * heads
    head_rows = half * 2 // heads
    groups = max(1, half // head_rows)
    total = [None] * groups
    for k in range(1, chips) if forward else range(chips - 1, 0, -1):
        used = (k <= chip) if forward else (k > chip)
        for g in range(groups):
            span = spans[0] if heads == 1 else jnp.where(core == 0, spans[g], spans[groups + g])
            factor = jnp.where(used, jnp.exp(span), 0.0)
            at = slice(g * half // groups, (g + 1) * half // groups)
            term = factor * messages[k - 1][at, :].astype(F32)
            total[g] = term if total[g] is None else total[g] + term
        spans = [span + foot for span, foot in zip(spans, feet[k - 1])]
    for g in range(groups):
        out[g * half // groups : (g + 1) * half // groups, :] = total[g].astype(BF16)


def enter(forward, heads, place, mine, theirs, other, out):
    core = place[1]
    half, width = mine.shape
    rows = 2 * half
    out[pl.ds(pl.multiple_of(core * half, half), half), :] = mine[...].astype(F32)
    out[pl.ds(pl.multiple_of((1 - core) * half, half), half), :] = theirs[...].astype(F32)
    totals = get_foot(other, rows, heads)
    late = core == (1 if forward else 0)
    for h in range(heads):
        at = slice(h * width, (h + 1) * width)
        now = out[at, :]
        moved = other[at, :].astype(F32) + jnp.exp(totals[h]) * now
        out[at, :] = jnp.where(late, moved, now)


def causal_mask(size):
    return lax.broadcasted_iota(jnp.int32, (size, size), 0) >= lax.broadcasted_iota(
        jnp.int32, (size, size), 1
    )


def decay_of(run, columns, r, causal):
    return jnp.exp(jnp.where(causal, columns[:, r : r + 1] - run[r : r + 1, :], -jnp.inf))


def local_body(queries, keys, values, tables, states, mixed, grown_rows):
    size = tables.shape[2]
    length, columns = mixed.shape
    chunks = length // size
    heads = tables.shape[1] // chunks
    width = columns // heads
    causal = causal_mask(size)
    run = tables[RUN]
    sums, grow = run.T, tables[GROW].T
    def step(h, j):
        cols, rows = slice(h * width, (h + 1) * width), slice(j * size, (j + 1) * size)
        r = j * heads + h
        query, key, value = queries[rows, cols], keys[rows, cols], values[rows, cols]
        scores = mm(query, key, NT)
        grown = (query * grow[:, r : r + 1]).astype(BF16)
        yield True
        weight = (scores * decay_of(run, sums, r, causal)).astype(BF16)
        turned = grown.T
        yield True
        out = mm(weight, value, NN)
        if j:
            at = slice((h * chunks + j) * width, (h * chunks + j + 1) * width)
            out = out + mm(grown, states[at, :], NN)
        yield True
        grown_rows[cols, rows] = turned
        mixed[rows, cols] = out
        yield True

    for h in range(heads):
        together(step(h, j) for j in range(chunks))
        grown_rows.send(h)


def norm_body(
    heads, place, mixed, queries, tables, mine, theirs, other, attended, inverse, incoming
):
    width = mine.shape[1]
    size = tables.shape[2]
    chunks = tables.shape[1] // heads
    enter(True, heads, place, mine, theirs, other, incoming)
    grow = tables[GROW_BLOCK].T
    ones = jnp.full((width, width), 1.0 / width, BF16)
    lane = lax.broadcasted_iota(jnp.int32, (size, width), 1)
    low = [incoming[h * width : (h + 1) * width, :].astype(BF16) for h in range(heads)]
    def step(j, h, scales):
        cols, rows = slice(h * width, (h + 1) * width), slice(j * size, (j + 1) * size)
        r = j * heads + h
        grown = (queries[rows, cols] * grow[:, r : r + 1]).astype(BF16)
        yield True
        total = mixed[rows, cols] + mm(grown, low[h], NN)
        square = (total * total).astype(BF16)
        yield True
        scale = lax.rsqrt(mm(square, ones, NN) + 1e-05)
        yield True
        scales[0] = jnp.where(lane == h, scale, scales[0])
        attended[rows, cols] = (total * scale).astype(BF16)
        yield True

    for j in range(chunks):
        scales = [jnp.zeros((size, width), F32)]
        together(step(j, h, scales) for h in range(heads))
        inverse[j * heads : (j + 1) * heads, :] = scales[0].T[:heads, :]
        attended.send(j)


def head_grad_body(size, weight, whole, out):
    for t in range(out.shape[0] // size):
        rows = slice(t * size, (t + 1) * size)
        out[rows, :] = mm(whole[rows, :], weight[...], NN)


def weight_copies(head, blocks, weight, rows_of_weight, semaphores):
    depth = rows_of_weight.shape[0] // len(blocks)
    return [
        pltpu.make_async_copy(
            weight.at[pl.ds(pl.multiple_of((head ^ k) * depth, depth), depth), :],
            rows_of_weight.at[i * depth : (i + 1) * depth, :],
            semaphores.at[i],
        )
        for i, k in enumerate(blocks)
    ]


def early_body(size, place, weight, attended, *refs):
    pieces, mine, theirs, out, rows_of_weight, semaphores = (
        refs[:3], refs[3], refs[4:7], refs[7], refs[8], refs[9]
    )
    _, core, _, head = place
    part = mine.shape[1]
    copies = weight_copies(head, (0, 1, 2), weight, rows_of_weight, semaphores)
    for copy in copies:
        copy.start()
    for i, piece in enumerate(pieces):
        product = mm(piece[...], attended[...], TN)
        low, high = product[:part, :].astype(BF16), product[part:, :].astype(BF16)
        mine[i] = jnp.where(core == 0, low, high)
        theirs[i][...] = jnp.where(core == 0, high, low)
    for copy in copies:
        copy.wait()
    for t in range(out.shape[0] // size):
        rows = slice(t * size, (t + 1) * size)
        out[rows, :] = sum(
            mm(piece[rows, :], rows_of_weight[2 * part * i : 2 * part * (i + 1), :], NN)
            for i, piece in enumerate(pieces)
        )


def late_body(heads, number, place, weight, attended, *refs):
    pieces = refs[:number]
    refs = refs[number:]
    partial, inverse, grown_rows, tables, mixed_grad, update, packed, exits = refs[:8]
    width = update.shape[1]
    size = tables.shape[2]
    chunks = tables.shape[1] // heads
    if number:
        mine, theirs, rows_of_weight, semaphores = refs[8:]
        _, core, _, head = place
        part = mine.shape[0]
        copy, = weight_copies(head, (3,), weight, rows_of_weight, semaphores)
        copy.start()
        low, high = [mm(p[...], attended[...], TN).astype(BF16) for p in pieces]
        mine[...] = jnp.where(core == 0, low, high)
        theirs[...] = jnp.where(core == 0, high, low)
        copy.wait()
    ones = jnp.full((width, width), 1.0 / width, BF16)
    states = [None] * heads
    run = tables[RUN]
    scales = inverse[...].T

    def step(j, h, total):
        cols, rows = slice(h * width, (h + 1) * width), slice(j * size, (j + 1) * size)
        r = j * heads + h
        grad = total[:, cols]
        unit = attended[rows, cols].astype(F32)
        both = (grad * unit).astype(BF16)
        yield True
        mean = mm(both, ones, NN)
        yield True
        grad = ((grad - unit * mean) * scales[:, r : r + 1]).astype(BF16)
        yield True
        term = mm(grown_rows[cols, rows], grad, NN)
        yield True
        mixed_grad[rows, cols] = grad
        at = slice((h * chunks + j) * width, (h * chunks + j + 1) * width)
        later = states[h]
        exits[at, :] = jnp.zeros((width, width), BF16) if later is None else later.astype(BF16)
        end = jnp.exp(run[r : r + 1, size - 1 : size])
        states[h] = term if later is None else term + later * end
        yield True

    for j in reversed(range(chunks)):
        rows = slice(j * size, (j + 1) * size)
        total = partial[rows, :]
        for i, piece in enumerate(pieces):
            total = total + mm(
                piece[rows, :], rows_of_weight[i * part : (i + 1) * part, :], NN
            )
        together(step(j, h, total) for h in range(heads))
    for h in range(heads):
        at = slice(h * width, (h + 1) * width)
        update[at, :] = states[h]
        packed[at, :] = states[h].astype(BF16)
    put_foot(packed, heads * width, block_totals(run, heads, width))


def back_body(
    heads, queries, keys, values, mixed_grad, tables, incoming, states, exits,
    query_grad, key_grad, value_grad,
):
    width = incoming.shape[1]
    size = tables.shape[2]
    chunks = tables.shape[1] // heads
    causal = lax.broadcasted_iota(jnp.int32, (size, size), 0) <= lax.broadcasted_iota(
        jnp.int32, (size, size), 1
    )
    below = causal_mask(size)
    run = tables[RUN]
    sums, grow, tails = run.T, tables[GROW].T, tables[TAIL].T

    def step(h, j, start):
        cols, rows = slice(h * width, (h + 1) * width), slice(j * size, (j + 1) * size)
        r = j * heads + h
        at = slice((h * chunks + j) * width, (h * chunks + j + 1) * width)
        grad, query = mixed_grad[rows, cols], queries[rows, cols]
        key, value = keys[rows, cols], values[rows, cols]
        weight, masked, turned = mm(key, query, NT), mm(value, grad, NT), mm(grad, value, NT)
        yield True
        decay = jnp.exp(
            jnp.where(causal, run[r : r + 1, :] - sums[:, r : r + 1], -jnp.inf)
        )
        weight, masked = (weight * decay).astype(BF16), (masked * decay).astype(BF16)
        yield True
        decay = jnp.exp(jnp.where(below, sums[:, r : r + 1] - run[r : r + 1, :], -jnp.inf))
        turned = (turned * decay).astype(BF16)
        grown = (grad * grow[:, r : r + 1]).astype(BF16)
        state = ((states[at, :].astype(F32) + start) if j else start).astype(BF16)
        if j < chunks - 1:
            tail = tails[:, r : r + 1]
            value_tail, key_tail = (value * tail).astype(BF16), (key * tail).astype(BF16)
        yield True
        query_part = mm(turned, key, NN) + mm(grown, state, NT)
        key_part = mm(masked, query, NN)
        value_part = mm(weight, grad, NN)
        if j < chunks - 1:
            key_part = key_part + mm(value_tail, exits[at, :], NT)
            value_part = value_part + mm(key_tail, exits[at, :], NN)
        yield True
        query_grad[rows, cols] = query_part.astype(BF16)
        key_grad[rows, cols] = key_part.astype(BF16)
        value_grad[rows, cols] = value_part.astype(BF16)
        yield True

    for h in range(heads):
        starts = [incoming[h * width : (h + 1) * width, :]]
        for j in range(1, chunks):
            r = (j - 1) * heads + h
            starts.append(starts[-1] * grow[size - 1 : size, r : r + 1])
        together(step(h, j, starts[j]) for j in range(chunks))
        query_grad.send(h)
        key_grad.send(h)
        value_grad.send(h)


def final_body(
    heads, place, keys, values, tables, mine, theirs, other, key_part, value_part,
    key_grad, value_grad, outgoing,
):
    width = mine.shape[1]
    size = tables.shape[2]
    chunks = tables.shape[1] // heads
    enter(False, heads, place, mine, theirs, other, outgoing)
    tails = tables[TAIL_BLOCK].T
    def step(h, j, state):
        cols, rows = slice(h * width, (h + 1) * width), slice(j * size, (j + 1) * size)
        r = j * heads + h
        tail = tails[:, r : r + 1]
        value_tail = (values[rows, cols] * tail).astype(BF16)
        key_tail = (keys[rows, cols] * tail).astype(BF16)
        yield True
        key_sum, value_sum = mm(value_tail, state, NT), mm(key_tail, state, NN)
        yield True
        key_grad[rows, cols] = (key_part[rows, cols] + key_sum).astype(BF16)
        value_grad[rows, cols] = (value_part[rows, cols] + value_sum).astype(BF16)
        yield True

    for h in range(heads):
        state = outgoing[h * width : (h + 1) * width, :].astype(BF16)
        together(step(h, j, state) for j in range(chunks))
        key_grad.send(h)
        value_grad.send(h)


def fold_body(place, mine, low, middle, high, kept, sent):
    odd = place[2] % 2 == 1
    parts = [
        (mine[i].astype(F32) + part[...].astype(F32)).astype(BF16)
        for i, part in enumerate((low, middle, high))
    ]
    kept[0] = jnp.where(odd, parts[1], parts[0])
    kept[1] = parts[2]
    sent[0] = jnp.where(odd, parts[0], parts[1])
    sent[1] = parts[2]


def fold_again_body(place, kept, arrived, total, sent):
    turn = place[2]
    first = kept[0].astype(F32) + arrived[0].astype(F32)
    second = kept[1].astype(F32) + arrived[1].astype(F32)
    total[...] = jnp.where(turn == 2, second, first)
    sent[...] = jnp.where(turn == 0, second, first).astype(BF16)


def add_body(mine, arrived, out):
    out[...] = (mine[...].astype(F32) + arrived[...].astype(F32)).astype(BF16)


def cut_body(span, block, out, token):
    out[...] = block[:, span]
    token[...] = jnp.zeros(token.shape, F32)


def hop(value, step, turns, chips, count):
    moves = [
        (s * count + y, ((s // 2 ^ step) * 2 + s % 2) * count + y)
        for s in range(2 * chips)
        for y in range(count)
        if s // 2 ^ y in turns
    ]
    return lax.ppermute(value, ("seq", "head"), moves)


class Chain:
    def __init__(self, line, forward, heads, chips, update, packed):
        self.line, self.forward, self.heads, self.chips = line, forward, heads, chips
        self.update, self.packed = update, packed
        self.other = self.swap(packed)

    def swap(self, value):
        return lax.ppermute(value, "seq", [(i, i ^ 1) for i in range(2 * self.chips)])

    def send(self):
        rows, width = self.update.shape
        self.half = (rows // 2, width)
        message, = self.line.call(
            functools.partial(combine_body, self.forward, self.heads),
            [((rows // 2 + foot_rows(self.heads), width), BF16)],
            self.update, self.packed, self.other,
            scratch=[pltpu.VMEM((rows, width), F32)], place=True,
        )
        self.line.held[self] = self.other
        self.arrived = [
            lax.ppermute(
                message, "seq",
                [(i, (i // 2 + k) % self.chips * 2 + i % 2) for i in range(2 * self.chips)],
            )
            for k in range(1, self.chips)
        ]

    def join(self):
        self.mine, = self.line.call(
            functools.partial(join_body, self.forward, self.heads, self.chips),
            [(self.half, BF16)], *self.arrived, place=True,
        )
        self.theirs = self.swap(self.mine)

    def done(self):
        self.line.held.pop(self)
        return self.mine, self.theirs, self.other


def on_device(seq_size, head_size, queries, keys, values, log_decay, out_weight, out_grad):
    length, columns = queries.shape
    heads = log_decay.shape[0]
    width = columns // heads
    size = 256 if length % 256 == 0 else length
    chunks = length // size
    chips = seq_size // 2
    near = head_size == 4 and chips == 4
    seq, head = lax.axis_index("seq"), lax.axis_index("head")
    turn = (seq // 2) ^ head
    block = out_grad.shape[1]
    part = block // 2
    move = lambda a, k: lax.ppermute(a, "head", [(i, i ^ k) for i in range(head_size)])
    if near:
        x, y = move(out_grad, 1), move(out_grad, 2)
    else:
        whole = lax.all_gather(out_grad, "head", axis=1, tiled=True)
    state = ((heads * width, width), F32)
    message = ((heads * width + foot_rows(heads), width), BF16)
    rows = (length, columns)
    line = Line()
    held = line.held

    chunk_states = ((heads * chunks * width, width), BF16)
    tables, update, packed, states = line.call(
        state_body, [((5, chunks * heads, size), F32), state, message, chunk_states],
        keys, values, log_decay, fetch={2: 1, 0: heads, 1: heads}, store={3: (heads, 0)},
    )
    forward = Chain(line, True, heads, chips, update, packed)
    pass
    forward.send()
    mixed, grown_rows = line.call(
        local_body, [(rows, F32), ((columns, length), BF16)], queries, keys, values, tables, states,
        fetch={0: heads, 1: heads, 2: heads, 4: (heads, 0)}, store={1: (heads, 0)},
    )
    held.update(mixed=mixed)
    forward.join()
    entering = forward.done()
    held.pop("mixed")
    attended, inverse, incoming = line.call(
        functools.partial(norm_body, heads),
        [(rows, BF16), ((chunks * heads, size), F32), state],
        mixed, queries, tables, *entering, place=True,
        fetch={1: (chunks, 0)}, store={0: (chunks, 0)},
    )
    held.update(inverse=inverse, incoming=incoming)
    swap = lambda a: lax.ppermute(a, "seq", [(i, i ^ 1) for i in range(2 * chips)])
    shape = (part, columns)
    if near:
        cut = [((length, part), BF16), ((8, 128), F32)]
        low, _ = line.call(functools.partial(cut_body, slice(0, part)), cut, x)
        diagonal = [move(low, 2)]
        high, _ = line.call(functools.partial(cut_body, slice(part, block)), cut, y)
        diagonal.append(move(high, 1))
        products, *theirs, partial = line.call(
            functools.partial(early_body, size),
            [((3,) + shape, BF16)] + [(shape, BF16)] * 3 + [(rows, F32)],
            out_weight, attended, out_grad, x, y,
            scratch=[pltpu.VMEM((3 * block, columns), BF16), pltpu.SemaphoreType.DMA((3,))],
            place=True, raw=(0,), fetch={1: 1, 2: 1, 3: 1, 4: 1}, loose=(3, 4),
        )
        arrived = [swap(a) for a in theirs]
        held["partial"] = partial
        kept, sent = line.call(
            fold_body, [((2,) + shape, BF16), ((2,) + shape, BF16)],
            products, *arrived, place=True,
        )
        arrived = hop(sent, 1, (0, 1, 2, 3), chips, head_size)
        held.pop("partial")
        mixed_grad, back_update, back_packed, exits, last, theirs = line.call(
            functools.partial(late_body, heads, 2),
            [(rows, BF16), state, message, chunk_states, (shape, BF16), (shape, BF16)],
            out_weight, attended, *diagonal, partial, inverse, grown_rows, tables,
            scratch=[pltpu.VMEM((block, columns), BF16), pltpu.SemaphoreType.DMA((1,))],
            place=True, raw=(0,), fetch={1: 1, 2: 1, 3: 1, 6: (1, 0)}, loose=(2, 3),
            store={3: (heads, 0)},
        )
        held["last"] = last
        last_arrived = swap(theirs)
    else:
        partial, = line.call(
            functools.partial(head_grad_body, size), [(rows, F32)],
            out_weight, whole,
        )
        mixed_grad, back_update, back_packed, exits = line.call(
            functools.partial(late_body, heads, 0), [(rows, BF16), state, message, chunk_states],
            out_weight, attended, partial, inverse, grown_rows, tables, place=True,
        )
    back = Chain(line, False, heads, chips, back_update, back_packed)
    held.pop("inverse")
    held["mixed_grad"] = mixed_grad
    held["update"] = back_update
    back.send()
    held.pop("update")
    if near:
        held.pop("last")
        last, = line.call(add_body, [(shape, BF16)], last, last_arrived)
        held["last"] = last
        last_arrived = hop(last, 1, (0, 2), chips, head_size)
        total, sent = line.call(
            fold_again_body, [(shape, F32), (shape, BF16)], kept, arrived, place=True,
        )
        arrived = hop(sent, 2, (0, 2, 3), chips, head_size)
    query_grad, key_part, value_part = line.call(
        functools.partial(back_body, heads), [(rows, BF16), (rows, BF16), (rows, BF16)],
        queries, keys, values, mixed_grad, tables, incoming, states, exits,
        fetch={0: heads, 1: heads, 2: heads, 6: (heads, 0), 7: (heads, 0)},
        store={i: heads for i in range(3)},
    )
    for name in ("mixed_grad", "incoming"):
        held.pop(name)
    back.join()
    if near:
        held.pop("last")
        last, = line.call(add_body, [(shape, BF16)], last, last_arrived)
        last_arrived = hop(last, 2, (1,), chips, head_size)
    key_grad, value_grad = line.call(
        functools.partial(final_body, heads), [(rows, BF16)] * 2,
        keys, values, tables, *back.done(), key_part, value_part,
        scratch=[pltpu.VMEM((heads * width, width), F32)], place=True,
        fetch={0: heads, 1: heads, 6: heads, 7: heads}, store={0: heads, 1: heads},
    )
    if near:
        weight_grad = jnp.where(
            turn == 3, last.astype(F32) + last_arrived.astype(F32),
            total + arrived.astype(F32),
        )
    else:
        weight_grad = lax.psum_scatter(
            mm(whole, attended, TN), "seq", scatter_dimension=0, tiled=True
        )
    return attended, query_grad, key_grad, value_grad, weight_grad.astype(BF16)


def solution(mesh):
    block = P("seq", "head")
    return jax.shard_map(
        functools.partial(on_device, mesh.shape["seq"], mesh.shape["head"]),
        mesh=mesh,
        in_specs=(block, block, block, P("head", "seq"), P(None, "head"), block),
        out_specs=(block,) * 5,
        check_vma=False,
    )
```

```python
import functools

import jax
import jax.numpy as jnp
from jax import lax
from jax.experimental import pallas as pl
from jax.experimental.pallas import tpu as pltpu
from jax.sharding import PartitionSpec as P

HIGH = lax.Precision.HIGHEST
F32 = jnp.float32
BF16 = jnp.bfloat16
VMEM = pl.BlockSpec(memory_space=pltpu.VMEM)
ANY = pl.BlockSpec(memory_space=pl.ANY)
NN = (((1,), (0,)), ((), ()))
NT = (((1,), (1,)), ((), ()))
TN = (((0,), (0,)), ((), ()))


def mm(left, right, dims):
    return lax.dot_general(left, right, dims, preferred_element_type=F32)


class Fetch:
    def __init__(self, source, buffer, semaphores, axis=1):
        self.buffer, self.axis = buffer, axis
        self.count = semaphores.shape[0]
        self.step = buffer.shape[axis] // self.count
        at = [
            (slice(None),) * axis + (slice(i * self.step, (i + 1) * self.step),)
            for i in range(self.count)
        ]
        self.copies = [
            pltpu.make_async_copy(source.at[p], buffer.at[p], semaphores.at[i])
            for i, p in enumerate(at)
        ]
        self.waiting = set(range(self.count))

        self.shape = buffer.shape

    def __getitem__(self, index):
        span = index[self.axis] if isinstance(index, tuple) else slice(None)
        first, last = span.start or 0, span.stop or self.buffer.shape[self.axis]
        wanted = {i for i in self.waiting if first < (i + 1) * self.step and i * self.step < last}
        if wanted and 0 not in self.waiting or len(wanted) > 1:
            wanted = set(self.waiting)
        for i in sorted(wanted):
            self.copies[i].wait()
        self.waiting -= wanted
        return self.buffer[index]


def start_all(*fetches):
    for i in range(max(f.count for f in fetches)):
        for f in fetches:
            if i < f.count:
                f.copies[i].start()


class Store(Fetch):
    def __init__(self, target, buffer, semaphores, axis=1):
        self.buffer, self.axis = buffer, axis
        self.count = semaphores.shape[0]
        self.step = buffer.shape[axis] // self.count
        at = [
            (slice(None),) * axis + (slice(i * self.step, (i + 1) * self.step),)
            for i in range(self.count)
        ]
        self.copies = [
            pltpu.make_async_copy(buffer.at[p], target.at[p], semaphores.at[i])
            for i, p in enumerate(at)
        ]

        self.shape, self.ready, self.left = buffer.shape, [], set(range(self.count))

    def __setitem__(self, index, value):
        self.buffer[index] = value

    def send(self, i):
        self.ready.append(i)
        if len(self.ready) * 2 >= self.count:
            self.start(self.ready)
            self.ready = []

    def start(self, blocks):
        for i in blocks:
            self.copies[i].start()
            self.left.remove(i)

    def finish(self):
        self.start(sorted(self.left))
        for copy in self.copies:
            copy.wait()


GROUP = 4


def together(steps):
    steps = list(steps)
    for i in range(0, len(steps), GROUP):
        running = steps[i : i + GROUP]
        while running:
            running = [step for step in running if next(step, None) is not None]


def here():
    seq, head = lax.axis_index("seq"), lax.axis_index("head")
    return seq >> 1, seq & 1, (seq >> 1) ^ head, head


class Line:
    def __init__(self):
        self.last = None
        self.held = {}

    def call(self, body, outs, *args, scratch=(), place=False, fetch={}, store={}, raw=(), raw_out=(), loose=()):
        fetch = {i: f if isinstance(f, tuple) else (f, 1) for i, f in fetch.items()}
        store = {i: f if isinstance(f, tuple) else (f, 1) for i, f in store.items()}
        shapes = [
            (pltpu.HBM if i in store or i in raw_out else jax.ShapeDtypeStruct)(shape, dtype)
            for i, (shape, dtype) in enumerate(outs)
        ]
        seen = {id(a) for a in args}
        extra = [] if self.last is None else [self.last]
        extra += [a for a in self.held.values()]
        extra = [a for a in extra if id(a) not in seen]
        count, more, results = len(args), len(extra), len(outs)
        hbm = pl.BlockSpec(memory_space=pltpu.HBM)
        specs = [ANY if i in loose else hbm if i in fetch else hbm if i in raw else VMEM for i in range(count)]
        buffers = []
        for i, (blocks, _) in fetch.items():
            buffers += [pltpu.VMEM(args[i].shape, args[i].dtype), pltpu.SemaphoreType.DMA((blocks,))]
        for i, (blocks, _) in store.items():
            buffers += [pltpu.VMEM(*outs[i]), pltpu.SemaphoreType.DMA((blocks,))]

        def kernel(*refs):
            ins, out = list(refs[:count]), list(refs[count + more : count + more + results])
            rest = list(refs[count + more + results :])
            for i, (_, axis) in fetch.items():
                ins[i] = Fetch(ins[i], rest.pop(0), rest.pop(0), axis)
            for i, (_, axis) in store.items():
                out[i] = Store(out[i], rest.pop(0), rest.pop(0), axis)
            if fetch:
                start_all(*[ins[i] for i in fetch])
            if place:
                ins = [here()] + ins
            body(*ins, *out, *rest)
            for i in store:
                out[i].finish()

        args = [
            pltpu.with_memory_space_constraint(a, pltpu.HBM) if (i in fetch or i in raw) and i not in loose else a
            for i, a in enumerate(args)
        ]
        values = pl.pallas_call(
            kernel,
            out_shape=shapes,
            in_specs=specs + [ANY] * more,
            out_specs=[hbm if i in store or i in raw_out else VMEM for i in range(results)],
            scratch_shapes=buffers + list(scratch),
            compiler_params=pltpu.CompilerParams(vmem_limit_bytes=24 * 1024 * 1024),
        )(*args, *extra)
        least = min(range(results), key=lambda i: values[i].size * values[i].dtype.itemsize)
        self.last = values[least]
        if least in store or least in raw_out:
            self.last = pltpu.with_memory_space_constraint(self.last, pltpu.HBM)
        return values


def foot_rows(heads):
    return -(-3 * heads // 16) * 16


def put_foot(out, base, totals):
    rows = []
    for total in totals:
        for _ in range(3):
            part = total.astype(BF16)
            rows.append(part.astype(F32))
            total = total - part.astype(F32)
    width = rows[0].shape[1]
    fill = foot_rows(len(totals)) - len(rows)
    if fill:
        rows.append(jnp.zeros((fill, width), F32))
    out[base:, :] = jnp.concatenate(rows, axis=0).astype(BF16)


def get_foot(message, base, heads):
    foot = message[base:, :].astype(F32)
    return [
        foot[3 * h : 3 * h + 1, :] + foot[3 * h + 1 : 3 * h + 2, :] + foot[3 * h + 2 : 3 * h + 3, :]
        for h in range(heads)
    ]


RUN, GROW, TAIL, GROW_BLOCK, TAIL_BLOCK = range(5)


def state_body(keys, values, log_decay, tables, update, packed, states):
    heads, size = log_decay.buffer.shape[0], tables.shape[2]
    chunks = tables.shape[1] // heads
    width = update.shape[1]
    upper = (
        lax.broadcasted_iota(jnp.int32, (size, size), 0)
        <= lax.broadcasted_iota(jnp.int32, (size, size), 1)
    ).astype(F32)
    pieces = jnp.concatenate(
        [log_decay[:, j * size : (j + 1) * size] for j in range(chunks)], axis=0
    )
    run = lax.dot_general(pieces, upper, NN, precision=HIGH, preferred_element_type=F32)
    ends = [run[j * heads : (j + 1) * heads, size - 1 : size] for j in range(chunks)]
    before, after = [jnp.zeros((heads, 1), F32)], [jnp.zeros((heads, 1), F32)]
    for j in range(chunks - 1):
        before.append(before[-1] + ends[j])
        after.append(after[-1] + ends[chunks - 1 - j])
    before = jnp.concatenate(before, axis=0)
    after = jnp.concatenate(after[::-1], axis=0)
    left = run[:, size - 1 : size] - run
    tables[RUN] = run
    tables[GROW] = jnp.exp(run)
    tables[TAIL] = jnp.exp(left)
    tables[GROW_BLOCK] = jnp.exp(run + before)
    tables[TAIL_BLOCK] = jnp.exp(left + after)
    tail_columns = jnp.exp(left).T
    def product(h, j, terms):
        cols, rows = slice(h * width, (h + 1) * width), slice(j * size, (j + 1) * size)
        r = j * heads + h
        tail = (keys[rows, cols] * tail_columns[:, r : r + 1]).astype(BF16)
        value = values[rows, cols]
        yield True
        terms.append(mm(tail, value, TN))
        yield True

    for h in range(heads):
        cols = slice(h * width, (h + 1) * width)
        terms = []
        together(product(h, j, terms) for j in range(chunks))
        state = None
        for j in range(chunks):
            r = j * heads + h
            at = slice((h * chunks + j) * width, (h * chunks + j + 1) * width)
            states[at, :] = jnp.zeros((width, width), BF16) if j == 0 else state.astype(BF16)
            end = jnp.exp(run[r : r + 1, size - 1 : size])
            state = terms[j] if state is None else state * end + terms[j]
        states.send(h)
        update[cols, :] = state
        packed[cols, :] = state.astype(BF16)
    put_foot(packed, heads * width, block_totals(run, heads, width))


def block_totals(run, heads, width):
    chunks, size = run.shape[0] // heads, run.shape[1]
    ends = run[:, size - 1 : size]
    return [
        sum(
            jnp.broadcast_to(ends[j * heads + h : j * heads + h + 1, :], (1, width))
            for j in range(chunks)
        )
        for h in range(heads)
    ]


def combine_body(forward, heads, place, own, packed, other, out, whole):
    core = place[1]
    width = own.shape[1]
    rows = heads * width
    mine, theirs = get_foot(packed, rows, heads), get_foot(other, rows, heads)
    late = core == (1 if forward else 0)
    for h in range(heads):
        at = slice(h * width, (h + 1) * width)
        a, b = own[at, :], other[at, :].astype(F32)
        joined = jnp.where(late, a + jnp.exp(mine[h]) * b, b + jnp.exp(theirs[h]) * a)
        whole[at, :] = joined
    half = rows // 2
    out[:half, :] = whole[pl.ds(pl.multiple_of(core * half, half), half), :].astype(BF16)
    put_foot(out, half, [a + b for a, b in zip(mine, theirs)])


def join_body(forward, heads, chips, place, *refs):
    messages, out = refs[: chips - 1], refs[chips - 1]
    chip, core = place[0], place[1]
    half, width = out.shape
    feet = [get_foot(m, half, heads) for m in messages]
    spans = [jnp.zeros((1, width), F32)] * heads
    head_rows = half * 2 // heads
    groups = max(1, half // head_rows)
    total = [None] * groups
    for k in range(1, chips) if forward else range(chips - 1, 0, -1):
        used = (k <= chip) if forward else (k > chip)
        for g in range(groups):
            span = spans[0] if heads == 1 else jnp.where(core == 0, spans[g], spans[groups + g])
            factor = jnp.where(used, jnp.exp(span), 0.0)
            at = slice(g * half // groups, (g + 1) * half // groups)
            term = factor * messages[k - 1][at, :].astype(F32)
            total[g] = term if total[g] is None else total[g] + term
        spans = [span + foot for span, foot in zip(spans, feet[k - 1])]
    for g in range(groups):
        out[g * half // groups : (g + 1) * half // groups, :] = total[g].astype(BF16)


def enter(forward, heads, place, mine, theirs, other, out):
    core = place[1]
    half, width = mine.shape
    rows = 2 * half
    out[pl.ds(pl.multiple_of(core * half, half), half), :] = mine[...].astype(F32)
    out[pl.ds(pl.multiple_of((1 - core) * half, half), half), :] = theirs[...].astype(F32)
    totals = get_foot(other, rows, heads)
    late = core == (1 if forward else 0)
    for h in range(heads):
        at = slice(h * width, (h + 1) * width)
        now = out[at, :]
        moved = other[at, :].astype(F32) + jnp.exp(totals[h]) * now
        out[at, :] = jnp.where(late, moved, now)


def causal_mask(size):
    return lax.broadcasted_iota(jnp.int32, (size, size), 0) >= lax.broadcasted_iota(
        jnp.int32, (size, size), 1
    )


def decay_of(run, columns, r, causal):
    return jnp.exp(jnp.where(causal, columns[:, r : r + 1] - run[r : r + 1, :], -jnp.inf))


def local_body(queries, keys, values, tables, states, mixed, grown_rows):
    size = tables.shape[2]
    length, columns = mixed.shape
    chunks = length // size
    heads = tables.shape[1] // chunks
    width = columns // heads
    causal = causal_mask(size)
    run = tables[RUN]
    sums, grow = run.T, tables[GROW].T
    def step(h, j):
        cols, rows = slice(h * width, (h + 1) * width), slice(j * size, (j + 1) * size)
        r = j * heads + h
        query, key, value = queries[rows, cols], keys[rows, cols], values[rows, cols]
        scores = mm(query, key, NT)
        grown = (query * grow[:, r : r + 1]).astype(BF16)
        yield True
        weight = (scores * decay_of(run, sums, r, causal)).astype(BF16)
        turned = grown.T
        yield True
        out = mm(weight, value, NN)
        if j:
            at = slice((h * chunks + j) * width, (h * chunks + j + 1) * width)
            out = out + mm(grown, states[at, :], NN)
        yield True
        grown_rows[cols, rows] = turned
        mixed[rows, cols] = out
        yield True

    for h in range(heads):
        together(step(h, j) for j in range(chunks))
        grown_rows.send(h)


def norm_body(
    heads, place, mixed, queries, tables, mine, theirs, other, attended, inverse, incoming
):
    width = mine.shape[1]
    size = tables.shape[2]
    chunks = tables.shape[1] // heads
    enter(True, heads, place, mine, theirs, other, incoming)
    grow = tables[GROW_BLOCK].T
    ones = jnp.full((width, width), 1.0 / width, BF16)
    lane = lax.broadcasted_iota(jnp.int32, (size, width), 1)
    low = [incoming[h * width : (h + 1) * width, :].astype(BF16) for h in range(heads)]
    def step(j, h, scales):
        cols, rows = slice(h * width, (h + 1) * width), slice(j * size, (j + 1) * size)
        r = j * heads + h
        grown = (queries[rows, cols] * grow[:, r : r + 1]).astype(BF16)
        yield True
        total = mixed[rows, cols] + mm(grown, low[h], NN)
        square = (total * total).astype(BF16)
        yield True
        scale = lax.rsqrt(mm(square, ones, NN) + 1e-05)
        yield True
        scales[0] = jnp.where(lane == h, scale, scales[0])
        attended[rows, cols] = (total * scale).astype(BF16)
        yield True

    for j in range(chunks):
        scales = [jnp.zeros((size, width), F32)]
        together(step(j, h, scales) for h in range(heads))
        inverse[j * heads : (j + 1) * heads, :] = scales[0].T[:heads, :]
        attended.send(j)


def head_grad_body(size, weight, whole, out):
    for t in range(out.shape[0] // size):
        rows = slice(t * size, (t + 1) * size)
        out[rows, :] = mm(whole[rows, :], weight[...], NN)


def weight_copies(head, blocks, weight, rows_of_weight, semaphores):
    depth = rows_of_weight.shape[0] // len(blocks)
    return [
        pltpu.make_async_copy(
            weight.at[pl.ds(pl.multiple_of((head ^ k) * depth, depth), depth), :],
            rows_of_weight.at[i * depth : (i + 1) * depth, :],
            semaphores.at[i],
        )
        for i, k in enumerate(blocks)
    ]


def early_body(size, place, weight, attended, *refs):
    pieces, mine, theirs, out, rows_of_weight, semaphores = (
        refs[:3], refs[3], refs[4:7], refs[7], refs[8], refs[9]
    )
    _, core, _, head = place
    part = mine.shape[1]
    copies = weight_copies(head, (0, 1, 2), weight, rows_of_weight, semaphores)
    for copy in copies:
        copy.start()
    for i, piece in enumerate(pieces):
        product = mm(piece[...], attended[...], TN)
        low, high = product[:part, :].astype(BF16), product[part:, :].astype(BF16)
        mine[i] = jnp.where(core == 0, low, high)
        theirs[i][...] = jnp.where(core == 0, high, low)
    for copy in copies:
        copy.wait()
    for t in range(out.shape[0] // size):
        rows = slice(t * size, (t + 1) * size)
        out[rows, :] = sum(
            mm(piece[rows, :], rows_of_weight[2 * part * i : 2 * part * (i + 1), :], NN)
            for i, piece in enumerate(pieces)
        )


def late_body(heads, number, place, weight, attended, *refs):
    pieces = refs[:number]
    refs = refs[number:]
    partial, inverse, grown_rows, tables, mixed_grad, update, packed, exits = refs[:8]
    width = update.shape[1]
    size = tables.shape[2]
    chunks = tables.shape[1] // heads
    if number:
        mine, theirs, rows_of_weight, semaphores = refs[8:]
        _, core, _, head = place
        part = mine.shape[0]
        copy, = weight_copies(head, (3,), weight, rows_of_weight, semaphores)
        copy.start()
        low, high = [mm(p[...], attended[...], TN).astype(BF16) for p in pieces]
        mine[...] = jnp.where(core == 0, low, high)
        theirs[...] = jnp.where(core == 0, high, low)
        copy.wait()
    ones = jnp.full((width, width), 1.0 / width, BF16)
    states = [None] * heads
    run = tables[RUN]
    scales = inverse[...].T

    def step(j, h, total):
        cols, rows = slice(h * width, (h + 1) * width), slice(j * size, (j + 1) * size)
        r = j * heads + h
        grad = total[:, cols]
        unit = attended[rows, cols].astype(F32)
        both = (grad * unit).astype(BF16)
        yield True
        mean = mm(both, ones, NN)
        yield True
        grad = ((grad - unit * mean) * scales[:, r : r + 1]).astype(BF16)
        yield True
        term = mm(grown_rows[cols, rows], grad, NN)
        yield True
        mixed_grad[rows, cols] = grad
        at = slice((h * chunks + j) * width, (h * chunks + j + 1) * width)
        later = states[h]
        exits[at, :] = jnp.zeros((width, width), BF16) if later is None else later.astype(BF16)
        end = jnp.exp(run[r : r + 1, size - 1 : size])
        states[h] = term if later is None else term + later * end
        yield True

    for j in reversed(range(chunks)):
        rows = slice(j * size, (j + 1) * size)
        total = partial[rows, :]
        for i, piece in enumerate(pieces):
            total = total + mm(
                piece[rows, :], rows_of_weight[i * part : (i + 1) * part, :], NN
            )
        together(step(j, h, total) for h in range(heads))
    for h in range(heads):
        at = slice(h * width, (h + 1) * width)
        update[at, :] = states[h]
        packed[at, :] = states[h].astype(BF16)
    put_foot(packed, heads * width, block_totals(run, heads, width))


def back_body(
    heads, queries, keys, values, mixed_grad, tables, incoming, states, exits,
    query_grad, key_grad, value_grad,
):
    width = incoming.shape[1]
    size = tables.shape[2]
    chunks = tables.shape[1] // heads
    causal = lax.broadcasted_iota(jnp.int32, (size, size), 0) <= lax.broadcasted_iota(
        jnp.int32, (size, size), 1
    )
    below = causal_mask(size)
    run = tables[RUN]
    sums, grow, tails = run.T, tables[GROW].T, tables[TAIL].T

    def step(h, j, start):
        cols, rows = slice(h * width, (h + 1) * width), slice(j * size, (j + 1) * size)
        r = j * heads + h
        at = slice((h * chunks + j) * width, (h * chunks + j + 1) * width)
        grad, query = mixed_grad[rows, cols], queries[rows, cols]
        key, value = keys[rows, cols], values[rows, cols]
        weight, masked, turned = mm(key, query, NT), mm(value, grad, NT), mm(grad, value, NT)
        yield True
        decay = jnp.exp(
            jnp.where(causal, run[r : r + 1, :] - sums[:, r : r + 1], -jnp.inf)
        )
        weight, masked = (weight * decay).astype(BF16), (masked * decay).astype(BF16)
        yield True
        decay = jnp.exp(jnp.where(below, sums[:, r : r + 1] - run[r : r + 1, :], -jnp.inf))
        turned = (turned * decay).astype(BF16)
        grown = (grad * grow[:, r : r + 1]).astype(BF16)
        state = ((states[at, :].astype(F32) + start) if j else start).astype(BF16)
        if j < chunks - 1:
            tail = tails[:, r : r + 1]
            value_tail, key_tail = (value * tail).astype(BF16), (key * tail).astype(BF16)
        yield True
        query_part = mm(
            jnp.concatenate([turned, grown], 1), jnp.concatenate([key, state.T], 0), NN
        )
        if j < chunks - 1:
            left = exits[at, :]
            masked = jnp.concatenate([masked, value_tail], 1)
            weight = jnp.concatenate([weight, key_tail], 1)
            query = jnp.concatenate([query, left.T], 0)
            grad = jnp.concatenate([grad, left], 0)
        key_part = mm(masked, query, NN)
        value_part = mm(weight, grad, NN)
        yield True
        query_grad[rows, cols] = query_part.astype(BF16)
        key_grad[rows, cols] = key_part.astype(BF16)
        value_grad[rows, cols] = value_part.astype(BF16)
        yield True

    for h in range(heads):
        starts = [incoming[h * width : (h + 1) * width, :]]
        for j in range(1, chunks):
            r = (j - 1) * heads + h
            starts.append(starts[-1] * grow[size - 1 : size, r : r + 1])
        together(step(h, j, starts[j]) for j in range(chunks))
        query_grad.send(h)
        key_grad.send(h)
        value_grad.send(h)


def final_body(
    heads, place, keys, values, tables, mine, theirs, other, key_part, value_part,
    key_grad, value_grad, outgoing,
):
    width = mine.shape[1]
    size = tables.shape[2]
    chunks = tables.shape[1] // heads
    enter(False, heads, place, mine, theirs, other, outgoing)
    tails = tables[TAIL_BLOCK].T
    def step(h, j, state):
        cols, rows = slice(h * width, (h + 1) * width), slice(j * size, (j + 1) * size)
        r = j * heads + h
        tail = tails[:, r : r + 1]
        value_tail = (values[rows, cols] * tail).astype(BF16)
        key_tail = (keys[rows, cols] * tail).astype(BF16)
        yield True
        key_sum, value_sum = mm(value_tail, state, NT), mm(key_tail, state, NN)
        yield True
        key_grad[rows, cols] = (key_part[rows, cols] + key_sum).astype(BF16)
        value_grad[rows, cols] = (value_part[rows, cols] + value_sum).astype(BF16)
        yield True

    for h in range(heads):
        state = outgoing[h * width : (h + 1) * width, :].astype(BF16)
        together(step(h, j, state) for j in range(chunks))
        key_grad.send(h)
        value_grad.send(h)


def fold_body(place, mine, low, middle, high, kept, sent):
    odd = place[2] % 2 == 1
    parts = [
        (mine[i].astype(F32) + part[...].astype(F32)).astype(BF16)
        for i, part in enumerate((low, middle, high))
    ]
    kept[0] = jnp.where(odd, parts[1], parts[0])
    kept[1] = parts[2]
    sent[0] = jnp.where(odd, parts[0], parts[1])
    sent[1] = parts[2]


def fold_again_body(place, kept, arrived, total, sent):
    turn = place[2]
    first = kept[0].astype(F32) + arrived[0].astype(F32)
    second = kept[1].astype(F32) + arrived[1].astype(F32)
    total[...] = jnp.where(turn == 2, second, first)
    sent[...] = jnp.where(turn == 0, second, first).astype(BF16)


def add_body(mine, arrived, out):
    out[...] = (mine[...].astype(F32) + arrived[...].astype(F32)).astype(BF16)


def cut_body(span, block, out, token):
    out[...] = block[:, span]
    token[...] = jnp.zeros(token.shape, F32)


def hop(value, step, turns, chips, count):
    moves = [
        (s * count + y, ((s // 2 ^ step) * 2 + s % 2) * count + y)
        for s in range(2 * chips)
        for y in range(count)
        if s // 2 ^ y in turns
    ]
    return lax.ppermute(value, ("seq", "head"), moves)


class Chain:
    def __init__(self, line, forward, heads, chips, update, packed):
        self.line, self.forward, self.heads, self.chips = line, forward, heads, chips
        self.update, self.packed = update, packed
        self.other = self.swap(packed)

    def swap(self, value):
        return lax.ppermute(value, "seq", [(i, i ^ 1) for i in range(2 * self.chips)])

    def send(self):
        rows, width = self.update.shape
        self.half = (rows // 2, width)
        message, = self.line.call(
            functools.partial(combine_body, self.forward, self.heads),
            [((rows // 2 + foot_rows(self.heads), width), BF16)],
            self.update, self.packed, self.other,
            scratch=[pltpu.VMEM((rows, width), F32)], place=True,
        )
        self.line.held[self] = self.other
        self.arrived = [
            lax.ppermute(
                message, "seq",
                [(i, (i // 2 + k) % self.chips * 2 + i % 2) for i in range(2 * self.chips)],
            )
            for k in range(1, self.chips)
        ]

    def join(self):
        self.mine, = self.line.call(
            functools.partial(join_body, self.forward, self.heads, self.chips),
            [(self.half, BF16)], *self.arrived, place=True,
        )
        self.theirs = self.swap(self.mine)

    def done(self):
        self.line.held.pop(self)
        return self.mine, self.theirs, self.other


def on_device(seq_size, head_size, queries, keys, values, log_decay, out_weight, out_grad):
    length, columns = queries.shape
    heads = log_decay.shape[0]
    width = columns // heads
    size = 256 if length % 256 == 0 else length
    chunks = length // size
    chips = seq_size // 2
    half = max(1, heads // 2)
    near = head_size == 4 and chips == 4
    seq, head = lax.axis_index("seq"), lax.axis_index("head")
    turn = (seq // 2) ^ head
    block = out_grad.shape[1]
    part = block // 2
    move = lambda a, k: lax.ppermute(a, "head", [(i, i ^ k) for i in range(head_size)])
    if near:
        x, y = move(out_grad, 1), move(out_grad, 2)
    else:
        whole = lax.all_gather(out_grad, "head", axis=1, tiled=True)
    state = ((heads * width, width), F32)
    message = ((heads * width + foot_rows(heads), width), BF16)
    rows = (length, columns)
    line = Line()
    held = line.held

    chunk_states = ((heads * chunks * width, width), BF16)
    tables, update, packed, states = line.call(
        state_body, [((5, chunks * heads, size), F32), state, message, chunk_states],
        keys, values, log_decay, fetch={2: 1, 0: heads, 1: heads}, store={3: (heads, 0)},
    )
    forward = Chain(line, True, heads, chips, update, packed)
    pass
    forward.send()
    mixed, grown_rows = line.call(
        local_body, [(rows, F32), ((columns, length), BF16)], queries, keys, values, tables, states,
        fetch={0: half, 1: half, 2: half, 4: (half, 0)}, store={1: (heads, 0)},
    )
    held.update(mixed=mixed)
    forward.join()
    entering = forward.done()
    held.pop("mixed")
    attended, inverse, incoming = line.call(
        functools.partial(norm_body, heads),
        [(rows, BF16), ((chunks * heads, size), F32), state],
        mixed, queries, tables, *entering, place=True,
        fetch={1: (chunks, 0)}, store={0: (chunks, 0)},
    )
    held.update(inverse=inverse, incoming=incoming)
    swap = lambda a: lax.ppermute(a, "seq", [(i, i ^ 1) for i in range(2 * chips)])
    shape = (part, columns)
    if near:
        cut = [((length, part), BF16), ((8, 128), F32)]
        low, _ = line.call(functools.partial(cut_body, slice(0, part)), cut, x)
        diagonal = [move(low, 2)]
        high, _ = line.call(functools.partial(cut_body, slice(part, block)), cut, y)
        diagonal.append(move(high, 1))
        products, *theirs, partial = line.call(
            functools.partial(early_body, size),
            [((3,) + shape, BF16)] + [(shape, BF16)] * 3 + [(rows, F32)],
            out_weight, attended, out_grad, x, y,
            scratch=[pltpu.VMEM((3 * block, columns), BF16), pltpu.SemaphoreType.DMA((3,))],
            place=True, raw=(0,), fetch={1: 1, 2: 1, 3: 1, 4: 1}, loose=(3, 4),
        )
        arrived = [swap(a) for a in theirs]
        held["partial"] = partial
        kept, sent = line.call(
            fold_body, [((2,) + shape, BF16), ((2,) + shape, BF16)],
            products, *arrived, place=True,
        )
        arrived = hop(sent, 1, (0, 1, 2, 3), chips, head_size)
        held.pop("partial")
        mixed_grad, back_update, back_packed, exits, last, theirs = line.call(
            functools.partial(late_body, heads, 2),
            [(rows, BF16), state, message, chunk_states, (shape, BF16), (shape, BF16)],
            out_weight, attended, *diagonal, partial, inverse, grown_rows, tables,
            scratch=[pltpu.VMEM((block, columns), BF16), pltpu.SemaphoreType.DMA((1,))],
            place=True, raw=(0,), fetch={1: 1, 2: 1, 3: 1, 6: (1, 0)}, loose=(2, 3),
            store={3: (heads, 0)},
        )
        held["last"] = last
        last_arrived = swap(theirs)
    else:
        partial, = line.call(
            functools.partial(head_grad_body, size), [(rows, F32)],
            out_weight, whole,
        )
        mixed_grad, back_update, back_packed, exits = line.call(
            functools.partial(late_body, heads, 0), [(rows, BF16), state, message, chunk_states],
            out_weight, attended, partial, inverse, grown_rows, tables, place=True,
        )
    back = Chain(line, False, heads, chips, back_update, back_packed)
    held.pop("inverse")
    held["mixed_grad"] = mixed_grad
    held["update"] = back_update
    back.send()
    held.pop("update")
    if near:
        held.pop("last")
        last, = line.call(add_body, [(shape, BF16)], last, last_arrived)
        held["last"] = last
        last_arrived = hop(last, 1, (0, 2), chips, head_size)
        total, sent = line.call(
            fold_again_body, [(shape, F32), (shape, BF16)], kept, arrived, place=True,
        )
        arrived = hop(sent, 2, (0, 2, 3), chips, head_size)
    query_grad, key_part, value_part = line.call(
        functools.partial(back_body, heads), [(rows, BF16), (rows, BF16), (rows, BF16)],
        queries, keys, values, mixed_grad, tables, incoming, states, exits,
        fetch={0: half, 1: half, 2: half, 6: (half, 0), 7: (half, 0)},
        store={i: heads for i in range(3)},
    )
    for name in ("mixed_grad", "incoming"):
        held.pop(name)
    back.join()
    if near:
        held.pop("last")
        last, = line.call(add_body, [(shape, BF16)], last, last_arrived)
        last_arrived = hop(last, 2, (1,), chips, head_size)
    key_grad, value_grad = line.call(
        functools.partial(final_body, heads), [(rows, BF16)] * 2,
        keys, values, tables, *back.done(), key_part, value_part,
        scratch=[pltpu.VMEM((heads * width, width), F32)], place=True,
        fetch={0: half, 1: half, 6: half, 7: half}, store={0: heads, 1: heads},
    )
    if near:
        weight_grad = jnp.where(
            turn == 3, last.astype(F32) + last_arrived.astype(F32),
            total + arrived.astype(F32),
        )
    else:
        weight_grad = lax.psum_scatter(
            mm(whole, attended, TN), "seq", scatter_dimension=0, tiled=True
        )
    return attended, query_grad, key_grad, value_grad, weight_grad.astype(BF16)


def solution(mesh):
    block = P("seq", "head")
    return jax.shard_map(
        functools.partial(on_device, mesh.shape["seq"], mesh.shape["head"]),
        mesh=mesh,
        in_specs=(block, block, block, P("head", "seq"), P(None, "head"), block),
        out_specs=(block,) * 5,
        check_vma=False,
    )
```
